32 devices in a mesh: groups: 2 (over y), seq: 4 (over z), mp: 4 (over x, core).
Axes of the slice: x: 2, y: 2, z: 4, core: 2. Of those that a mesh axis runs over, the one named last changes fastest.
Arguments:
- node_vectors: bfloat16 [1024, 2048], P(('groups', 'seq'), 'mp'), parts along dimension 0, may hold values from -6 to 6
- standardize_multiplier: float32 [2048], replicated, may hold values from 0.1 to 1.9
- probe_matrix: bfloat16 [2048, 1024], P(None, 'mp'), may hold values from -1 to 1
- lookup_matrix: bfloat16 [2048, 1024], P(None, 'mp'), may hold values from -1 to 1
- content_matrix: bfloat16 [2048, 1024], P(None, 'mp'), may hold values from -0.125 to 0.125
- softness_per_group: float32 [8], P('mp'), may hold values from 0.5 to 12
- exit_matrix: bfloat16 [1024, 2048], P('mp'), may hold values from -0.1875 to 0.1875
Outputs:
- mixed: bfloat16 [1024, 2048], P(('groups', 'seq'), 'mp'), parts along dimension 0
The draws below stay inside these ranges and needn't reach their ends.
There are 2 independent parts, one for each index of `groups`. The reference program is written for one: setup_inputs(seed, part) draws one part's arguments, and reference() takes and returns one part's arrays. A program takes and returns all parts, laid end to end along the dimension named above; an argument that names none is the same for every part. Nothing has to cross between parts.
All inputs are finite; a program needn't handle non-finite values.
Results may differ from the reference program's by a relative error of at most 0.011.
Values may be sent and summed in bfloat16 or wider, within the bound.
No kernel may reach another device: no remote copies, remote signals or barrier semaphores. Data moves between devices by JAX's collectives and lax.ppermute only.
A program may use at most 64 MiB of HBM per device.

```python
import math
import jax
import jax.numpy as jnp
from jax import lax

D = 2048
HEADS = 8
CHANNEL_SPAN = 128
LENGTH = 512


def draw_node_vectors(key, part):
    drawn = jax.random.normal(jax.random.fold_in(key, 21), (LENGTH, D), jnp.float32)
    return jnp.clip(drawn, -6.0, 6.0).astype(jnp.bfloat16)


def query_matrix(key):
    return jax.random.normal(jax.random.fold_in(key, 31), (D, HEADS * CHANNEL_SPAN), jnp.float32) / math.sqrt(D)


def draw_probe_matrix(key, part):
    return jnp.clip(query_matrix(key), -1.0, 1.0).astype(jnp.bfloat16)


def draw_lookup_matrix(key, part):
    drawn = jax.random.normal(jax.random.fold_in(key, 32), (D, HEADS * CHANNEL_SPAN), jnp.float32) / math.sqrt(D)
    return jnp.clip(drawn, -1.0, 1.0).astype(jnp.bfloat16)


def draw_softness_per_group(key, part):
    uniform_draw = jax.random.uniform(jax.random.fold_in(key, 41), (HEADS,), jnp.float32)
    return jnp.power(4.0, uniform_draw)


def block_scale(own_key, dims, shards, smallest, top_value):
    loudness = 1.0
    for dim, parts in shards:
        steps = jax.random.uniform(jax.random.fold_in(jax.random.fold_in(own_key, 6), dim), (parts,), jnp.float32, smallest / len(shards), top_value / len(shards))
        loudness = loudness * jnp.repeat(jnp.exp(steps), dims[dim] // parts).reshape((-1,) + (1,) * (len(dims) - 1 - dim))
    return loudness


def scatter_about(stream_key, shape, width, most, cuts=(), dtype=jnp.bfloat16):
    entries = jax.random.normal(stream_key, shape, jnp.float32) * width
    if len(cuts) > 0:
        entries = block_scale(stream_key, shape, cuts, -0.22, 0.18) * entries
    return jnp.clip(entries, min=-most, max=most).astype(dtype)


def setup_inputs(seed: int = 0, part: int = 0) -> dict:
    key_list = jax.random.split(jax.random.key(seed), 8)
    own_keys = jax.random.split(jax.random.fold_in(key_list[7], part), 8)
    node_vectors = draw_node_vectors(jax.random.fold_in(jax.random.fold_in(key_list[7], part), 71), part)
    standardize_multiplier = jnp.clip(1.0 + 0.18 * jax.random.normal(key_list[1], (D,), jnp.float32), 0.1, 1.9)
    probe_matrix = draw_probe_matrix(jax.random.fold_in(key_list[7], 71), part)
    lookup_matrix = draw_lookup_matrix(jax.random.fold_in(key_list[7], 71), part)
    content_matrix = scatter_about(key_list[4], (D, HEADS * CHANNEL_SPAN), D ** -0.5, 0.125, ((1, 4),))
    softness_per_group = draw_softness_per_group(jax.random.fold_in(key_list[7], 71), part)
    exit_matrix = scatter_about(key_list[6], (HEADS * CHANNEL_SPAN, D), (HEADS * CHANNEL_SPAN) ** -0.5, 0.1875, ((0, 4),))
    return dict(node_vectors=node_vectors, standardize_multiplier=standardize_multiplier, probe_matrix=probe_matrix, lookup_matrix=lookup_matrix, content_matrix=content_matrix, softness_per_group=softness_per_group, exit_matrix=exit_matrix)


def reference(node_vectors, standardize_multiplier, probe_matrix, lookup_matrix, content_matrix, softness_per_group, exit_matrix):
    widened = node_vectors.astype(jnp.float32)
    average = lax.optimization_barrier(jnp.mean(widened, axis=-1, keepdims=True))
    centered = widened - average
    variance = lax.optimization_barrier(jnp.mean(centered * centered, axis=-1, keepdims=True))
    normed = (centered * lax.rsqrt(variance + 1e-05) * standardize_multiplier).astype(jnp.bfloat16)
    queries = jnp.dot(normed, probe_matrix, preferred_element_type=jnp.float32).astype(jnp.bfloat16)
    key_rows = jnp.dot(normed, lookup_matrix, preferred_element_type=jnp.float32).astype(jnp.bfloat16)
    value_rows = jnp.dot(normed, content_matrix, preferred_element_type=jnp.float32).astype(jnp.bfloat16)
    query_heads = queries.reshape(LENGTH, HEADS, CHANNEL_SPAN).transpose(1, 0, 2)
    key_heads = key_rows.reshape(LENGTH, HEADS, CHANNEL_SPAN).transpose(1, 0, 2)
    value_heads = value_rows.reshape(LENGTH, HEADS, CHANNEL_SPAN).transpose(1, 0, 2)
    inverse_root_span = softness_per_group / math.sqrt(CHANNEL_SPAN)
    block_rows = math.gcd(LENGTH, 1024)

    def one_head(inputs):
        head_queries, head_keys, head_values, head_factor = inputs

        def one_block(query_block):
            scores = jnp.dot(query_block, head_keys.T, preferred_element_type=jnp.float32) * head_factor
            row_max = lax.optimization_barrier(jnp.max(scores, axis=-1, keepdims=True))
            weights = jnp.exp(scores - row_max)
            totals = lax.optimization_barrier(jnp.sum(weights, axis=-1, keepdims=True))
            attended = jnp.dot(weights.astype(jnp.bfloat16), head_values, preferred_element_type=jnp.float32)
            return attended / totals
        blocks = head_queries.reshape(LENGTH // block_rows, block_rows, CHANNEL_SPAN)
        return lax.map(one_block, blocks).reshape(LENGTH, CHANNEL_SPAN)
    attended = lax.map(one_head, (query_heads, key_heads, value_heads, inverse_root_span))
    heads_out = attended.transpose(1, 0, 2).reshape(LENGTH, HEADS * CHANNEL_SPAN).astype(jnp.bfloat16)
    projected = jnp.dot(heads_out, exit_matrix, preferred_element_type=jnp.float32)
    return (widened + projected).astype(jnp.bfloat16)
```

```python
import math

import jax
import jax.numpy as jnp
from jax import lax
from jax.sharding import PartitionSpec as P


def swap(block, axis, count, distance):
    return lax.ppermute(block, axis, [(i, i ^ distance) for i in range(count)])


def gather_blocks(block, axis, count):
    blocks = {0: block}
    distance = count // 2
    while distance:
        blocks.update({k ^ distance: swap(b, axis, count, distance) for k, b in list(blocks.items())})
        distance //= 2
    return [blocks[k] for k in range(count)]


def attend(query_heads, key_rows, value_rows, factor, channel_span):
    heads = query_heads.shape[1]
    count = key_rows.shape[0]
    key_heads = key_rows.reshape(count, heads, channel_span)
    value_heads = value_rows.reshape(count, heads, channel_span)
    scores = (
        jnp.einsum("rhd,nhd->hrn", query_heads, key_heads, preferred_element_type=jnp.float32)
        * factor[:, None, None]
    )
    weights = jnp.exp(scores - jnp.max(scores, axis=-1, keepdims=True))
    totals = jnp.sum(weights, axis=-1)
    weighted = jnp.einsum(
        "hrn,nhd->hrd",
        weights.astype(jnp.bfloat16),
        value_heads,
        preferred_element_type=jnp.float32,
    )
    return weighted / totals[:, :, None]


def per_device(mesh, node_vectors, gain, probe, lookup, content, softness, exit_matrix):
    mp, seq = mesh.shape["mp"], mesh.shape["seq"]
    me = lax.axis_index("mp")
    full_rows = lax.all_gather(node_vectors, "mp", axis=1, tiled=True)
    widened = full_rows.astype(jnp.float32)
    average = jnp.mean(widened, axis=-1, keepdims=True)
    centered = widened - average
    variance = jnp.mean(centered * centered, axis=-1, keepdims=True)
    normed = (centered * lax.rsqrt(variance + 1e-05) * gain).astype(jnp.bfloat16)
    key_rows = jnp.dot(normed, lookup, preferred_element_type=jnp.float32).astype(jnp.bfloat16)
    value_rows = jnp.dot(normed, content, preferred_element_type=jnp.float32).astype(jnp.bfloat16)
    queries = jnp.dot(normed, probe, preferred_element_type=jnp.float32).astype(jnp.bfloat16)
    heads = softness.shape[0]
    head_cols = queries.shape[1]
    channel_span = head_cols // heads
    rows = queries.shape[0]
    both = jnp.concatenate([key_rows, value_rows], axis=1)
    all_rows = jnp.concatenate(gather_blocks(both, "seq", seq), axis=0)
    heads_out = (
        attend(
            queries.reshape(rows, heads, channel_span),
            all_rows[:, :head_cols],
            all_rows[:, head_cols:],
            softness / math.sqrt(channel_span),
            channel_span,
        )
        .transpose(1, 0, 2)
        .reshape(rows, head_cols)
        .astype(jnp.bfloat16)
    )
    partial = jnp.dot(heads_out, exit_matrix, preferred_element_type=jnp.float32)
    width = partial.shape[1] // mp
    shares = {
        k: lax.dynamic_slice_in_dim(partial, (me ^ k) * width, width, axis=1) for k in range(mp)
    }
    distance = 1
    while distance < mp:
        shares = {
            k: shares[k]
            + swap(shares[k ^ distance].astype(jnp.bfloat16), "mp", mp, distance).astype(jnp.float32)
            for k in shares
            if not k & distance
        }
        distance *= 2
    return (node_vectors.astype(jnp.float32) + shares[0]).astype(jnp.bfloat16)


def solution(mesh):
    return jax.shard_map(
        lambda *arrays: per_device(mesh, *arrays),
        mesh=mesh,
        in_specs=(
            P(("groups", "seq"), "mp"),
            P(),
            P(None, "mp"),
            P(None, "mp"),
            P(None, "mp"),
            P("mp"),
            P("mp", None),
        ),
        out_specs=P(("groups", "seq"), "mp"),
        check_vma=False,
    )
```

```python
import functools
import math

import jax
import jax.numpy as jnp
from jax import lax
from jax.experimental import pallas as pl
from jax.experimental.pallas import tpu as pltpu
from jax.sharding import PartitionSpec as P

F32, BF16 = jnp.float32, jnp.bfloat16
VMEM = pl.BlockSpec(memory_space=pltpu.VMEM)
HBM = pl.BlockSpec(memory_space=pltpu.HBM)
PARAMS = pltpu.CompilerParams(vmem_limit_bytes=16 << 20)
LANES = 128


def swap(block, axis, count, distance):
    return lax.ppermute(block, axis, [(i, i ^ distance) for i in range(count)])


def after(value, *others):
    return lax.optimization_barrier((value, *others))[0]


def prepare_kernel(mp, heads, gain_ref, probe_ref, lookup_ref, content_ref, exit_ref, *refs):
    groups = mp.bit_length() - 1
    weights_ref, sums_ref, gain_out_ref, own_ref = refs[:4]
    far_refs = refs[4 : 4 + groups]
    rows_ref, sems, gain_sem, exit_sems = refs[4 + groups :]
    me = lax.axis_index("mp")
    depth, cols = probe_ref.shape
    parts = sems.shape[0]
    chunk = depth // parts
    gain_copy = pltpu.make_async_copy(gain_ref, gain_out_ref, gain_sem)
    gain_copy.start()
    copies = []
    for c in range(parts):
        rows = pl.ds(c * chunk, chunk)
        moves = [(probe_ref, 0, cols, 0)]
        for h in range(heads):
            moves.append((lookup_ref, h * LANES, LANES, cols + 2 * h * LANES))
            moves.append((content_ref, h * LANES, LANES, cols + (2 * h + 1) * LANES))
        copies.append([])
        for i, (ref, start, width, to) in enumerate(moves):
            copy = pltpu.make_async_copy(
                ref.at[rows, pl.ds(start, width)], weights_ref.at[rows, pl.ds(to, width)], sems.at[c, i]
            )
            copy.start()
            copies[c].append(copy)
    width = own_ref.shape[1]
    exits = []
    for k in range(mp):
        to = far_refs[k.bit_length() - 1].at[k - (1 << (k.bit_length() - 1))] if k else own_ref
        columns = pl.ds(pl.multiple_of((me ^ k) * width, width), width)
        exits.append(pltpu.make_async_copy(exit_ref.at[:, columns], to, exit_sems.at[k]))
        exits[k].start()
    gain_copy.wait()
    gain = gain_out_ref[...]
    high = gain.astype(BF16)
    rows_ref[...] = jnp.zeros_like(rows_ref)
    rows_ref[0:1, :] = high
    rows_ref[16:17, :] = (gain - high.astype(F32)).astype(BF16)
    for c in range(parts):
        for copy in copies[c]:
            copy.wait()
        span = pl.ds(c * chunk, chunk)
        part = jnp.dot(rows_ref[:, span], weights_ref[span, :], preferred_element_type=F32)
        part = part[0:8, :] + part[16:24, :]
        if c == 0:
            sums_ref[...] = part
        else:
            sums_ref[...] += part
    for copy in exits:
        copy.wait()


def prepare(mp, heads, gain, probe, lookup, content, exit_matrix):
    depth, cols = probe.shape
    deep, wide = exit_matrix.shape
    parts = 4
    groups = mp.bit_length() - 1
    out_shape = [
        pltpu.VMEM((depth, 3 * cols), BF16),
        pltpu.VMEM((8, 3 * cols), F32),
        pltpu.VMEM((1, depth), F32),
        pltpu.VMEM((deep, wide // mp), BF16),
    ] + [pltpu.VMEM((1 << i, deep, wide // mp), BF16) for i in range(groups)]
    weights, sums, gain, own, *far = pl.pallas_call(
        functools.partial(prepare_kernel, mp, heads),
        out_shape=out_shape,
        in_specs=[HBM] * 5,
        out_specs=[VMEM] * len(out_shape),
        scratch_shapes=[
            pltpu.VMEM((32, depth), BF16),
            pltpu.SemaphoreType.DMA((parts, 1 + 2 * heads)),
            pltpu.SemaphoreType.DMA,
            pltpu.SemaphoreType.DMA((mp,)),
        ],
        compiler_params=PARAMS,
        cost_estimate=pl.CostEstimate(
            flops=16 * depth * 3 * cols, bytes_accessed=18 * depth * cols, transcendentals=0
        ),
        name="prepare",
    )(
        *(
            pltpu.with_memory_space_constraint(w, pltpu.HBM)
            for w in (gain[None, :], probe, lookup, content, exit_matrix)
        )
    )
    return weights, sums, gain, own, far


def scaled_blocks(blocks, shift, gain_ref):
    me = lax.axis_index("mp")
    found = []
    for k, block in enumerate(blocks):
        width = block.shape[1]
        gain = gain_ref[0:1, pl.ds(pl.multiple_of((me ^ k) * width, width), width)]
        found.append(((block[...].astype(F32) - shift) * gain).astype(BF16))
    return found


def matmul(blocks, weights_ref, start, width):
    me = lax.axis_index("mp")
    total = None
    for k, block in enumerate(blocks):
        depth = block.shape[1]
        w = weights_ref[pl.ds(pl.multiple_of((me ^ k) * depth, depth), depth), pl.ds(start, width)]
        part = jnp.dot(block[...], w, preferred_element_type=F32)
        total = part if total is None else total + part
    return total


def first_kernel(count, start, *refs):
    blocks = refs[:count]
    weights_ref, sums_ref, gain_ref, out_ref, offset_ref, scale_ref, *scaled_refs = refs[count:]
    rows, width = blocks[0].shape
    depth = count * width
    shift = jnp.mean(blocks[0][...].astype(F32), axis=1, keepdims=True)
    scaled = scaled_blocks(blocks, shift, gain_ref)
    for value, ref in zip(scaled, scaled_refs):
        ref[...] = value
    total = matmul(scaled, weights_ref, start, out_ref.shape[1])
    one = jnp.zeros((rows, 1), F32)
    two = jnp.zeros((rows, 1), F32)
    for block in blocks:
        moved = block[...].astype(F32) - shift
        one += jnp.sum(moved, axis=1, keepdims=True)
        two += jnp.sum(moved * moved, axis=1, keepdims=True)
    offset = one / depth
    scale = lax.rsqrt(two / depth - offset * offset + 1e-05)
    out_ref[...] = (scale * (total - offset * sums_ref[0:1, pl.ds(start, out_ref.shape[1])])).astype(BF16)
    offset_ref[...] = jnp.broadcast_to(offset, offset_ref.shape)
    scale_ref[...] = jnp.broadcast_to(scale, scale_ref.shape)


def query_kernel(count, cols, *refs):
    blocks = refs[:count]
    weights_ref, sums_ref, offset_ref, scale_ref, factor_ref, q_ref = refs[count:]
    total = matmul(blocks, weights_ref, 0, cols)
    total -= offset_ref[:, 0:1] * sums_ref[0:1, 0:cols]
    q_ref[...] = (scale_ref[:, 0:1] * factor_ref[...] * total).astype(BF16)


def project(blocks, weights, sums, gain, factor):
    rows, width = blocks[0].shape
    cols = weights.shape[1] // 3
    pairs, offset, scale, *scaled = pl.pallas_call(
        functools.partial(first_kernel, len(blocks), cols),
        out_shape=[
            pltpu.VMEM((rows, 2 * cols), BF16),
            pltpu.VMEM((rows, LANES), F32),
            pltpu.VMEM((rows, LANES), F32),
        ]
        + [pltpu.VMEM(b.shape, BF16) for b in blocks],
        in_specs=[VMEM] * (len(blocks) + 3),
        out_specs=[VMEM] * (3 + len(blocks)),
        compiler_params=PARAMS,
        name="keys_values",
    )(*blocks, weights, sums, gain)
    queries = pl.pallas_call(
        functools.partial(query_kernel, len(blocks), cols),
        out_shape=pltpu.VMEM((rows, cols), BF16),
        in_specs=[VMEM] * (len(blocks) + 5),
        out_specs=VMEM,
        compiler_params=PARAMS,
        cost_estimate=pl.CostEstimate(
            flops=16 * rows * weights.size, bytes_accessed=4 * weights.size, transcendentals=0
        ),
        name="queries",
    )(*scaled, weights, sums, offset, scale, factor)
    return queries, pairs


def attend_kernel(count, heads, q_ref, *refs):
    blocks, out_ref = refs[:count], refs[count]
    for h in range(heads):
        q = q_ref[:, pl.ds(h * LANES, LANES)]
        key, value = pl.ds(2 * h * LANES, LANES), pl.ds((2 * h + 1) * LANES, LANES)
        scores = [
            lax.dot_general(q, b[:, key], (((1,), (1,)), ((), ())), preferred_element_type=F32)
            for b in blocks
        ]
        top = functools.reduce(jnp.maximum, [jnp.max(s, axis=1, keepdims=True) for s in scores])
        total, weighted = 0.0, 0.0
        for s, b in zip(scores, blocks):
            weights = jnp.exp2(s - top)
            total += jnp.sum(weights, axis=1, keepdims=True)
            weighted += jnp.dot(weights.astype(BF16), b[:, value], preferred_element_type=F32)
        out_ref[:, pl.ds(h * LANES, LANES)] = (weighted / total).astype(BF16)


def attend(heads, queries, blocks):
    if len(blocks) > 8:
        merged = jnp.concatenate(blocks, axis=0)
        blocks = [merged[i : i + 1024] for i in range(0, merged.shape[0], 1024)]
    return pl.pallas_call(
        functools.partial(attend_kernel, len(blocks), heads),
        out_shape=pltpu.VMEM(queries.shape, BF16),
        in_specs=[VMEM] * (len(blocks) + 1),
        out_specs=VMEM,
        compiler_params=pltpu.CompilerParams(vmem_limit_bytes=(48 if len(blocks) > 4 else 16) << 20),
        name="attend",
    )(queries, *blocks)


def finish_kernel(count, x_ref, *refs):
    mixed, exits, out_ref = refs[:count], refs[count:-1], refs[-1]
    total = x_ref[...].astype(F32)
    for value, e in zip(mixed, exits):
        total += jnp.dot(value[...], e[...], preferred_element_type=F32)
    out_ref[...] = total.astype(out_ref.dtype)


def per_device(mesh, node_vectors, gain, probe, lookup, content, softness, exit_matrix):
    mp, seq = mesh.shape["mp"], mesh.shape["seq"]
    heads = softness.shape[0]
    cols = probe.shape[1]
    span = cols // heads
    factor = jnp.repeat(softness * (math.log2(math.e) / math.sqrt(span)), span)[None, :]

    weights, sums, gains, own, far = prepare(mp, heads, gain, probe, lookup, content, exit_matrix)
    blocks = {0: node_vectors}
    distance = mp // 2
    while distance:
        new = {k ^ distance: swap(b, "mp", mp, distance) for k, b in blocks.items()}
        if distance == mp // 2:
            new, sums = lax.optimization_barrier((new, sums))
        blocks.update(new)
        distance //= 2
    blocks = [blocks[k] for k in range(mp)]

    queries, pairs = project(blocks, weights, sums, gains, factor)
    found = {0: pairs}
    distance = seq // 2
    while distance:
        new = {}
        for k, b in found.items():
            if k == 0 and distance < seq // 2:
                b = after(b, queries)
            new[k ^ distance] = swap(b, "seq", seq, distance)
        found.update(new)
        distance //= 2
    attended = attend(heads, queries, [found[k] for k in range(seq)])

    pieces, pending = {0: own}, {1 << i: [(0, f)] for i, f in enumerate(far)}
    distance = mp // 2
    while distance:
        for r, stack in pending[distance]:
            if distance < mp // 2:
                stack = after(stack, attended)
            moved = swap(stack, "mp", mp, distance)
            pieces[r ^ distance] = moved[0]
            low = 1
            while low < distance:
                pending[low].append((r ^ distance, moved[low : 2 * low]))
                low *= 2
        distance //= 2

    mixed = {k: swap(attended, "mp", mp, k) if k else attended for k in range(mp)}
    return pl.pallas_call(
        functools.partial(finish_kernel, mp),
        out_shape=jax.ShapeDtypeStruct(node_vectors.shape, node_vectors.dtype),
        in_specs=[VMEM] * (1 + 2 * mp),
        out_specs=VMEM,
        compiler_params=PARAMS,
        name="finish",
    )(node_vectors, *(mixed[k] for k in range(mp)), *(pieces[k] for k in range(mp)))


def solution(mesh):
    return jax.shard_map(
        lambda *arrays: per_device(mesh, *arrays),
        mesh=mesh,
        in_specs=(
            P(("groups", "seq"), "mp"),
            P(),
            P(None, "mp"),
            P(None, "mp"),
            P(None, "mp"),
            P("mp"),
            P("mp", None),
        ),
        out_specs=P(("groups", "seq"), "mp"),
        check_vma=False,
    )
```

```python
import functools
import math

import jax
import jax.numpy as jnp
from jax import lax
from jax.experimental import pallas as pl
from jax.experimental.pallas import tpu as pltpu
from jax.sharding import PartitionSpec as P

F32, BF16 = jnp.float32, jnp.bfloat16
VMEM = pl.BlockSpec(memory_space=pltpu.VMEM)
HBM = pl.BlockSpec(memory_space=pltpu.HBM)
LANES = 128


def call(kernel, name, out_shape, operands, work=0, limit=16, specs=None, scratch=()):
    return pl.pallas_call(
        kernel,
        out_shape=out_shape,
        in_specs=specs or [VMEM] * len(operands),
        out_specs=[VMEM] * len(out_shape),
        scratch_shapes=scratch,
        compiler_params=pltpu.CompilerParams(vmem_limit_bytes=limit << 20),
        cost_estimate=pl.CostEstimate(flops=work, bytes_accessed=work // 64, transcendentals=0),
        name=name,
    )(*operands)


def swap(block, axis, count, distance):
    return lax.ppermute(block, axis, [(i, i ^ distance) for i in range(count)])


def after(value, *others):
    return lax.optimization_barrier((value, *others))[0]


def prepare_kernel(mp, gain_ref, probe_ref, lookup_ref, content_ref, exit_ref, *refs):
    weight_refs, (sums_ref, gain_out_ref, own_ref, far_ref) = refs[:3], refs[3:7]
    rows_ref, sems, gain_sem, exit_sems = refs[7:]
    me = lax.axis_index("mp")
    depth, cols = probe_ref.shape
    parts = sems.shape[0]
    chunk = depth // parts
    gain_copy = pltpu.make_async_copy(gain_ref, gain_out_ref, gain_sem)
    gain_copy.start()
    copies = []
    for c in range(parts):
        rows = pl.ds(c * chunk, chunk)
        copies.append([])
        for i, ref in enumerate((probe_ref, lookup_ref, content_ref)):
            copy = pltpu.make_async_copy(ref.at[rows, :], weight_refs[i].at[rows, :], sems.at[c, i])
            copy.start()
            copies[c].append(copy)
    half, _, width = own_ref.shape
    exits = []
    for k in range(mp):
        to = own_ref.at[k] if k < half else far_ref.at[k - half]
        columns = pl.ds(pl.multiple_of((me ^ k) * width, width), width)
        exits.append(pltpu.make_async_copy(exit_ref.at[:, columns], to, exit_sems.at[k]))
        exits[k].start()
    gain_copy.wait()
    gain = gain_out_ref[...]
    high = gain.astype(BF16)
    rows_ref[...] = jnp.zeros_like(rows_ref)
    rows_ref[0:1, :] = high
    rows_ref[16:17, :] = (gain - high.astype(F32)).astype(BF16)
    for c in range(parts):
        for copy in copies[c]:
            copy.wait()
        span = pl.ds(c * chunk, chunk)
        for i, ref in enumerate(weight_refs):
            part = jnp.dot(rows_ref[:, span], ref[span, :], preferred_element_type=F32)
            part = part[0:8, :] + part[16:24, :]
            if c == 0:
                sums_ref[i] = part
            else:
                sums_ref[i] += part
    for copy in exits:
        copy.wait()


def prepare(mp, gain, probe, lookup, content, exit_matrix):
    depth, cols = probe.shape
    deep, wide = exit_matrix.shape
    parts = 4
    stack = pltpu.VMEM((mp // 2, deep, wide // mp), BF16)
    probe, lookup, content, sums, gain, own, far = call(
        functools.partial(prepare_kernel, mp),
        "prepare",
        [pltpu.VMEM((depth, cols), BF16)] * 3
        + [pltpu.VMEM((3, 8, cols), F32), pltpu.VMEM((1, depth), F32), stack, stack],
        [
            pltpu.with_memory_space_constraint(w, pltpu.HBM)
            for w in (gain[None, :], probe, lookup, content, exit_matrix)
        ],
        work=48 * depth * cols,
        specs=[HBM] * 5,
        scratch=[
            pltpu.VMEM((32, depth), BF16),
            pltpu.SemaphoreType.DMA((parts, 3)),
            pltpu.SemaphoreType.DMA,
            pltpu.SemaphoreType.DMA((mp,)),
        ],
    )
    return (probe, lookup, content), sums, gain, own, far


def matmul(blocks, places, weight_ref):
    me = lax.axis_index("mp")
    total = None
    for k, block in zip(places, blocks):
        depth = block.shape[1]
        w = weight_ref[pl.ds(pl.multiple_of((me ^ k) * depth, depth), depth), :]
        part = jnp.dot(block[...], w, preferred_element_type=F32)
        total = part if total is None else total + part
    return total


def take_in(blocks, places, shift, gain_ref, scaled_refs, weight_refs):
    me = lax.axis_index("mp")
    one, two, scaled = 0.0, 0.0, []
    for k, block, ref in zip(places, blocks, scaled_refs):
        width = block.shape[1]
        gain = gain_ref[0:1, pl.ds(pl.multiple_of((me ^ k) * width, width), width)]
        moved = block[...].astype(F32) - shift
        value = (moved * gain).astype(BF16)
        ref[...] = value
        scaled.append(value)
        one += jnp.sum(moved, axis=1, keepdims=True)
        two += jnp.sum(moved * moved, axis=1, keepdims=True)
    return one, two, [matmul(scaled, places, ref) for ref in weight_refs]


def early_kernel(places, *refs):
    count = len(places)
    blocks = refs[:count]
    lookup_ref, content_ref, gain_ref, stats_ref, keys_ref, values_ref = refs[count : count + 6]
    scaled_refs = refs[count + 6 :]
    shift = jnp.mean(blocks[0][...].astype(F32), axis=1, keepdims=True)
    one, two, (keys, values) = take_in(
        blocks, places, shift, gain_ref, scaled_refs, (lookup_ref, content_ref)
    )
    keys_ref[...] = keys
    values_ref[...] = values
    for i, value in enumerate((shift, one, two)):
        stats_ref[i] = jnp.broadcast_to(value, stats_ref.shape[1:])


def late_kernel(places, depth, *refs):
    count = len(places)
    blocks = refs[:count]
    lookup_ref, content_ref, gain_ref, sums_ref, stats_ref, keys_ref, values_ref = refs[count : count + 7]
    out_ref, final_ref, *scaled_refs = refs[count + 7 :]
    one, two, products = take_in(
        blocks, places, stats_ref[0, :, 0:1], gain_ref, scaled_refs, (lookup_ref, content_ref)
    )
    offset = (one + stats_ref[1, :, 0:1]) / depth
    scale = lax.rsqrt((two + stats_ref[2, :, 0:1]) / depth - offset * offset + 1e-05)
    for i, (product, ref) in enumerate(zip(products, (keys_ref, values_ref))):
        product = product + ref[...]
        product = (scale * (product - offset * sums_ref[i + 1, 0:1, :])).astype(BF16)
        for h in range(product.shape[1] // LANES):
            out_ref[:, pl.ds((2 * h + i) * LANES, LANES)] = product[:, h * LANES : (h + 1) * LANES]
    final_ref[0] = jnp.broadcast_to(offset, final_ref.shape[1:])
    final_ref[1] = jnp.broadcast_to(scale, final_ref.shape[1:])


def query_kernel(count, *refs):
    blocks = refs[:count]
    probe_ref, sums_ref, final_ref, factor_ref, q_ref = refs[count:]
    total = matmul(blocks, range(count), probe_ref) - final_ref[0, :, 0:1] * sums_ref[0, 0:1, :]
    q_ref[...] = (final_ref[1, :, 0:1] * factor_ref[...] * total).astype(BF16)


def project(blocks, weights, sums, gain, factor):
    rows, width = blocks[0].shape
    probe, lookup, content = weights
    cols = probe.shape[1]
    count = len(blocks)
    product = pltpu.VMEM((rows, cols), F32)
    block = pltpu.VMEM((rows, width), BF16)
    stats, keys, values, *scaled = call(
        functools.partial(early_kernel, range(count - 1)),
        "early",
        [pltpu.VMEM((3, rows, LANES), F32), product, product] + [block] * (count - 1),
        [*blocks[:-1], lookup, content, gain],
        work=16 * rows * probe.size,
    )
    pairs, final, last = call(
        functools.partial(late_kernel, range(count - 1, count), count * width),
        "late",
        [pltpu.VMEM((rows, 2 * cols), BF16), pltpu.VMEM((2, rows, LANES), F32), block],
        [blocks[-1], lookup, content, gain, sums, stats, keys, values],
    )
    (queries,) = call(
        functools.partial(query_kernel, count),
        "queries",
        [pltpu.VMEM((rows, cols), BF16)],
        [*scaled, last, probe, sums, final, factor],
        work=4 * rows * probe.size,
    )
    return queries, pairs


def attend_kernel(count, heads, q_ref, *refs):
    blocks, out_ref = refs[:count], refs[count]
    scores, tops, totals, weighted = [], [], [], []
    for h in range(heads):
        q = q_ref[:, pl.ds(h * LANES, LANES)]
        scores.append(
            [
                lax.dot_general(
                    q, b[:, pl.ds(2 * h * LANES, LANES)], (((1,), (1,)), ((), ())), preferred_element_type=F32
                )
                for b in blocks
            ]
        )
    for parts in scores:
        widest = functools.reduce(jnp.maximum, parts)
        tops.append(jnp.max(widest, axis=1, keepdims=True))
    weights = [[jnp.exp2(s - top) for s in parts] for parts, top in zip(scores, tops)]
    for h in range(heads):
        weighted.append(
            sum(
                jnp.dot(
                    w.astype(BF16), b[:, pl.ds((2 * h + 1) * LANES, LANES)], preferred_element_type=F32
                )
                for w, b in zip(weights[h], blocks)
            )
        )
        totals.append(jnp.sum(functools.reduce(jnp.add, weights[h]), axis=1, keepdims=True))
    for h in range(heads):
        out_ref[:, pl.ds(h * LANES, LANES)] = (weighted[h] / totals[h]).astype(BF16)


def attend(heads, queries, blocks):
    if len(blocks) > 8:
        merged = jnp.concatenate(blocks, axis=0)
        size = math.gcd(merged.shape[0], 1024)
        blocks = [merged[i : i + size] for i in range(0, merged.shape[0], size)]
    size = sum(b.shape[0] for b in blocks)
    (out,) = call(
        functools.partial(attend_kernel, len(blocks), heads),
        "attend",
        [pltpu.VMEM(queries.shape, BF16)],
        [queries, *blocks],
        limit=48 if size > 2048 else 16,
    )
    return out


def own_kernel(x_ref, mixed_ref, exit_ref, *out_refs):
    for k, ref in enumerate(out_refs):
        part = jnp.dot(mixed_ref[...], exit_ref[k], preferred_element_type=F32)
        ref[...] = part + x_ref[...].astype(F32) if k == 0 else part


def add_kernel(mixed_ref, exit_ref, *refs):
    count = len(refs) // 2
    for k in range(count):
        part = jnp.dot(mixed_ref[...], exit_ref[k], preferred_element_type=F32)
        refs[count + k][...] = (refs[k][...] + part).astype(refs[count + k].dtype)


def per_device(mesh, node_vectors, gain, probe, lookup, content, softness, exit_matrix):
    mp, seq = mesh.shape["mp"], mesh.shape["seq"]
    heads = softness.shape[0]
    cols = probe.shape[1]
    span = cols // heads
    top = mp // 2
    factor = jnp.repeat(softness * (math.log2(math.e) / math.sqrt(span)), span)[None, :]

    weights, sums, gains, own, far = prepare(mp, gain, probe, lookup, content, exit_matrix)
    blocks = {0: node_vectors}
    distance = top
    while distance:
        new = {k ^ distance: swap(b, "mp", mp, distance) for k, b in blocks.items()}
        if distance == top:
            new, sums = lax.optimization_barrier((new, sums))
        blocks.update(new)
        distance //= 2
    queries, pairs = project([blocks[k] for k in range(mp)], weights, sums, gains, factor)
    theirs = swap(far, "mp", mp, top)

    found = {0: pairs}
    distance = seq // 2
    while distance:
        new = {}
        for k, b in found.items():
            if k == 0 and distance < seq // 2:
                b = after(b, queries)
            new[k ^ distance] = swap(b, "seq", seq, distance)
        found.update(new)
        distance //= 2
    mixed = attend(heads, after(queries, theirs), [found[k] for k in range(seq)])

    rows, width = node_vectors.shape
    product, half = pltpu.VMEM((rows, width), F32), pltpu.VMEM((rows, width), BF16)
    mixed_far = swap(mixed, "mp", mp, top)
    parts = call(
        own_kernel, "own", [product] * top, [node_vectors, mixed, own], work=64 * rows * own.size
    )
    sent = call(add_kernel, "sent", [half] * (top - 1), [mixed_far, theirs[1:], *parts[1:]])
    (kept,) = call(
        add_kernel, "kept", [product], [mixed_far, theirs[:1], parts[0]], work=64 * rows * own.size
    )
    shares = {0: kept, **{k: sent[k - 1] for k in range(1, top)}}
    distance = 1
    while distance < top:
        shares = {
            k: shares[k].astype(F32)
            + swap(shares[k ^ distance].astype(BF16), "mp", mp, distance).astype(F32)
            for k in shares
            if not k & distance
        }
        distance *= 2
    return shares[0].astype(node_vectors.dtype)


def solution(mesh):
    return jax.shard_map(
        lambda *arrays: per_device(mesh, *arrays),
        mesh=mesh,
        in_specs=(
            P(("groups", "seq"), "mp"),
            P(),
            P(None, "mp"),
            P(None, "mp"),
            P(None, "mp"),
            P("mp"),
            P("mp", None),
        ),
        out_specs=P(("groups", "seq"), "mp"),
        check_vma=False,
    )
```

```python
import functools
import math

import jax
import jax.numpy as jnp
from jax import lax
from jax.experimental import pallas as pl
from jax.experimental.pallas import tpu as pltpu
from jax.sharding import PartitionSpec as P

F32, BF16 = jnp.float32, jnp.bfloat16
VMEM = pl.BlockSpec(memory_space=pltpu.VMEM)
HBM = pl.BlockSpec(memory_space=pltpu.HBM)
LANES = 128


def call(kernel, name, out_shape, operands, work=0, limit=16, specs=None, scratch=()):
    return pl.pallas_call(
        kernel,
        out_shape=out_shape,
        in_specs=specs or [VMEM] * len(operands),
        out_specs=[VMEM] * len(out_shape),
        scratch_shapes=scratch,
        compiler_params=pltpu.CompilerParams(vmem_limit_bytes=limit << 20),
        cost_estimate=pl.CostEstimate(flops=work, bytes_accessed=work // 64, transcendentals=0),
        name=name,
    )(*operands)


def swap(block, axis, count, distance):
    return lax.ppermute(block, axis, [(i, i ^ distance) for i in range(count)])


def after(value, *others):
    return lax.optimization_barrier((value, *others))[0]


def prepare_kernel(mp, gain_ref, probe_ref, lookup_ref, content_ref, exit_ref, *refs):
    weight_refs, (sums_ref, gain_out_ref, own_ref, far_ref) = refs[:3], refs[3:7]
    rows_ref, sems, gain_sem, exit_sems = refs[7:]
    me = lax.axis_index("mp")
    depth, cols = probe_ref.shape
    parts = sems.shape[0]
    chunk = depth // parts
    gain_copy = pltpu.make_async_copy(gain_ref, gain_out_ref, gain_sem)
    gain_copy.start()
    copies = []
    for c in range(parts):
        rows = pl.ds(c * chunk, chunk)
        copies.append([])
        for i, ref in enumerate((probe_ref, lookup_ref, content_ref)):
            copy = pltpu.make_async_copy(ref.at[rows, :], weight_refs[i].at[rows, :], sems.at[c, i])
            copy.start()
            copies[c].append(copy)
    half, _, width = own_ref.shape
    exits = []
    for k in range(mp):
        to = own_ref.at[k] if k < half else far_ref.at[k - half]
        columns = pl.ds(pl.multiple_of((me ^ k) * width, width), width)
        exits.append(pltpu.make_async_copy(exit_ref.at[:, columns], to, exit_sems.at[k]))
        exits[k].start()
    gain_copy.wait()
    gain = gain_out_ref[...]
    high = gain.astype(BF16)
    rows_ref[...] = jnp.zeros_like(rows_ref)
    rows_ref[0:1, :] = high
    rows_ref[16:17, :] = (gain - high.astype(F32)).astype(BF16)
    for c in range(parts):
        for copy in copies[c]:
            copy.wait()
        span = pl.ds(c * chunk, chunk)
        for i, ref in enumerate(weight_refs):
            part = jnp.dot(rows_ref[:, span], ref[span, :], preferred_element_type=F32)
            part = part[0:8, :] + part[16:24, :]
            if c == 0:
                sums_ref[i] = part
            else:
                sums_ref[i] += part
    for copy in exits:
        copy.wait()


def prepare(mp, gain, probe, lookup, content, exit_matrix):
    depth, cols = probe.shape
    deep, wide = exit_matrix.shape
    parts = 4
    stack = pltpu.VMEM((mp // 2, deep, wide // mp), BF16)
    probe, lookup, content, sums, gain, own, far = call(
        functools.partial(prepare_kernel, mp),
        "prepare",
        [pltpu.VMEM((depth, cols), BF16)] * 3
        + [pltpu.VMEM((3, 8, cols), F32), pltpu.VMEM((1, depth), F32), stack, stack],
        [
            pltpu.with_memory_space_constraint(w, pltpu.HBM)
            for w in (gain[None, :], probe, lookup, content, exit_matrix)
        ],
        work=48 * depth * cols,
        specs=[HBM] * 5,
        scratch=[
            pltpu.VMEM((32, depth), BF16),
            pltpu.SemaphoreType.DMA((parts, 3)),
            pltpu.SemaphoreType.DMA,
            pltpu.SemaphoreType.DMA((mp,)),
        ],
    )
    return (probe, lookup, content), sums, gain, own, far


def matmul(blocks, places, weight_ref):
    me = lax.axis_index("mp")
    total = None
    for k, block in zip(places, blocks):
        depth = block.shape[1]
        w = weight_ref[pl.ds(pl.multiple_of((me ^ k) * depth, depth), depth), :]
        part = jnp.dot(block[...], w, preferred_element_type=F32)
        total = part if total is None else total + part
    return total


def take_in(blocks, places, shift, gain_ref, scaled_refs, weight_refs):
    me = lax.axis_index("mp")
    one, two, scaled = 0.0, 0.0, []
    for k, block, ref in zip(places, blocks, scaled_refs):
        width = block.shape[1]
        gain = gain_ref[0:1, pl.ds(pl.multiple_of((me ^ k) * width, width), width)]
        moved = block[...].astype(F32) - shift
        value = (moved * gain).astype(BF16)
        ref[...] = value
        scaled.append(value)
        one += jnp.sum(moved, axis=1, keepdims=True)
        two += jnp.sum(moved * moved, axis=1, keepdims=True)
    return one, two, [matmul(scaled, places, ref) for ref in weight_refs]


def early_kernel(places, *refs):
    count = len(places)
    blocks = refs[:count]
    lookup_ref, content_ref, gain_ref, stats_ref, keys_ref, values_ref = refs[count : count + 6]
    scaled_refs = refs[count + 6 :]
    shift = jnp.mean(blocks[0][...].astype(F32), axis=1, keepdims=True)
    one, two, (keys, values) = take_in(
        blocks, places, shift, gain_ref, scaled_refs, (lookup_ref, content_ref)
    )
    keys_ref[...] = keys
    values_ref[...] = values
    for i, value in enumerate((shift, one, two)):
        stats_ref[i] = jnp.broadcast_to(value, stats_ref.shape[1:])


def parity():
    return lax.rem(lax.axis_index("seq"), 2)


def late_kernel(places, depth, *refs):
    count = len(places)
    blocks = refs[:count]
    lookup_ref, content_ref, gain_ref, sums_ref, stats_ref, keys_ref, values_ref = refs[count : count + 7]
    mine_ref, other_ref, final_ref, *scaled_refs = refs[count + 7 :]
    one, two, products = take_in(
        blocks, places, stats_ref[0, :, 0:1], gain_ref, scaled_refs, (lookup_ref, content_ref)
    )
    offset = (one + stats_ref[1, :, 0:1]) / depth
    scale = lax.rsqrt((two + stats_ref[2, :, 0:1]) / depth - offset * offset + 1e-05)
    first = parity() == 0
    for i, (product, ref) in enumerate(zip(products, (keys_ref, values_ref))):
        product = product + ref[...]
        product = scale * (product - offset * sums_ref[i + 1, 0:1, :])
        half = product.shape[1] // 2
        low, high = product[:, :half], product[:, half:]
        for out_ref, part in (
            (mine_ref, jnp.where(first, low, high)),
            (other_ref, jnp.where(first, high, low)),
        ):
            part = part.astype(BF16)
            for h in range(half // LANES):
                out_ref[:, pl.ds((2 * h + i) * LANES, LANES)] = part[:, h * LANES : (h + 1) * LANES]
    final_ref[0] = jnp.broadcast_to(offset, final_ref.shape[1:])
    final_ref[1] = jnp.broadcast_to(scale, final_ref.shape[1:])


def query_kernel(count, *refs):
    blocks = refs[:count]
    probe_ref, sums_ref, final_ref, factor_ref, other_ref, mine_ref, bundle_ref = refs[count:]
    total = matmul(blocks, range(count), probe_ref) - final_ref[0, :, 0:1] * sums_ref[0, 0:1, :]
    total = final_ref[1, :, 0:1] * factor_ref[...] * total
    half = total.shape[1] // 2
    low, high = total[:, :half], total[:, half:]
    first = parity() == 0
    mine_ref[...] = jnp.where(first, low, high).astype(BF16)
    bundle_ref[:, pl.ds(0, 2 * half)] = other_ref[...]
    bundle_ref[:, pl.ds(2 * half, half)] = jnp.where(first, high, low).astype(BF16)


def project(blocks, weights, sums, gain, factor):
    rows, width = blocks[0].shape
    probe, lookup, content = weights
    cols = probe.shape[1]
    count = len(blocks)
    product = pltpu.VMEM((rows, cols), F32)
    block = pltpu.VMEM((rows, width), BF16)
    stats, keys, values, *scaled = call(
        functools.partial(early_kernel, range(count - 1)),
        "early",
        [pltpu.VMEM((3, rows, LANES), F32), product, product] + [block] * (count - 1),
        [*blocks[:-1], lookup, content, gain],
        work=16 * rows * probe.size,
    )
    pair = pltpu.VMEM((rows, cols), BF16)
    mine, other, final, last = call(
        functools.partial(late_kernel, range(count - 1, count), count * width),
        "late",
        [pair, pair, pltpu.VMEM((2, rows, LANES), F32), block],
        [blocks[-1], lookup, content, gain, sums, stats, keys, values],
    )
    queries, bundle = call(
        functools.partial(query_kernel, count),
        "queries",
        [pltpu.VMEM((rows, cols // 2), BF16), pltpu.VMEM((rows, 3 * cols // 2), BF16)],
        [*scaled, last, probe, sums, final, factor, other],
        work=16 * rows * probe.size,
    )
    return queries, mine, other, bundle


def merge_kernel(*refs):
    rows = refs[0].shape[0]
    for i, ref in enumerate(refs[:-1]):
        refs[-1][pl.ds(i * rows, rows), :] = ref[...]


def attend_kernel(count, mine_ref, bundle_ref, *refs):
    blocks, out_refs = refs[:count], refs[count:]
    half = mine_ref.shape[1]
    rows = mine_ref.shape[0]
    for h in range(half // LANES):
        q = jnp.concatenate(
            [mine_ref[:, pl.ds(h * LANES, LANES)], bundle_ref[:, pl.ds(2 * half + h * LANES, LANES)]], axis=0
        )
        scores = [
            lax.dot_general(
                q, b[:, pl.ds(2 * h * LANES, LANES)], (((1,), (1,)), ((), ())), preferred_element_type=F32
            )
            for b in blocks
        ]
        top = functools.reduce(jnp.maximum, [jnp.max(s, axis=1, keepdims=True) for s in scores])
        weights = [jnp.exp2(s - top) for s in scores]
        weighted = sum(
            jnp.dot(
                w.astype(BF16), b[:, pl.ds((2 * h + 1) * LANES, LANES)], preferred_element_type=F32
            )
            for w, b in zip(weights, blocks)
        )
        total = sum(jnp.sum(w, axis=1, keepdims=True) for w in weights)
        out = (weighted / total).astype(BF16)
        for i, ref in enumerate(out_refs):
            ref[:, pl.ds(h * LANES, LANES)] = out[i * rows : (i + 1) * rows, :]


def attend(queries, bundle, blocks):
    rows, wide = blocks[0].shape
    (merged,) = call(
        merge_kernel,
        "merge",
        [pltpu.VMEM((len(blocks) * rows, wide), BF16)],
        blocks,
        work=10000 * rows * wide * len(blocks),
    )
    size = merged.shape[0]
    return call(
        functools.partial(attend_kernel, 2),
        "attend",
        [pltpu.VMEM(queries.shape, BF16)] * 2,
        [queries, bundle, bundle, merged],
        limit=56 if size > 2048 else 16,
    )


def own_kernel(x_ref, mixed_ref, exit_ref, *out_refs):
    deep = mixed_ref.shape[1]
    rows = pl.ds(pl.multiple_of(parity() * deep, deep), deep)
    for k, ref in enumerate(out_refs):
        part = jnp.dot(mixed_ref[...], exit_ref[k, rows, :], preferred_element_type=F32)
        ref[...] = part + x_ref[...].astype(F32) if k == 0 else part


def add_kernel(which, flips, *refs):
    count, values = len(which), len(flips)
    for i, k in enumerate(which):
        total = refs[2 * values + i][...]
        for j, flip in enumerate(flips):
            deep = refs[j].shape[1]
            at = 1 - parity() if flip else parity()
            rows = pl.ds(pl.multiple_of(at * deep, deep), deep)
            total += jnp.dot(refs[j][...], refs[values + j][k, rows, :], preferred_element_type=F32)
        out_ref = refs[2 * values + count + i]
        out_ref[...] = total.astype(out_ref.dtype)


def per_device(mesh, node_vectors, gain, probe, lookup, content, softness, exit_matrix):
    mp, seq = mesh.shape["mp"], mesh.shape["seq"]
    heads = softness.shape[0]
    cols = probe.shape[1]
    span = cols // heads
    top = mp // 2
    factor = jnp.repeat(softness * (math.log2(math.e) / math.sqrt(span)), span)[None, :]

    weights, sums, gains, own, far = prepare(mp, gain, probe, lookup, content, exit_matrix)
    blocks = {0: node_vectors}
    distance = top
    while distance:
        new = {k ^ distance: swap(b, "mp", mp, distance) for k, b in blocks.items()}
        if distance == top:
            new, sums = lax.optimization_barrier((new, sums))
        blocks.update(new)
        distance //= 2
    queries, mine, other, bundle = project(
        [blocks[k] for k in range(mp)], weights, sums, gains, factor
    )
    theirs = swap(far, "mp", mp, top)

    found = {0: mine}
    for k in sorted(range(1, seq), key=lambda k: (k == 1, k)):
        found[k] = swap(bundle if k == 1 else other if k % 2 else mine, "seq", seq, k)
    mixed, mixed_beside = attend(queries, found[1], [found[k] for k in range(seq) if k != 1])

    rows, width = node_vectors.shape
    product, half = pltpu.VMEM((rows, width), F32), pltpu.VMEM((rows, width), BF16)
    both = ("seq", "mp")
    across = swap(mixed, both, seq * mp, top)
    beside = swap(mixed_beside, both, seq * mp, mp)
    corner = swap(mixed_beside, both, seq * mp, mp + top)
    parts = call(
        own_kernel, "own", [product] * top, [node_vectors, mixed, own], work=1 * rows * own.size
    )
    parts = call(
        functools.partial(add_kernel, range(top), (0, 1)),
        "crossed",
        [product] * top,
        [across, corner, theirs, theirs, *parts],
        work=64 * rows * own.size,
    )
    sent = call(
        functools.partial(add_kernel, range(1, top), (1,)), "sent", [half] * (top - 1), [beside, own, *parts[1:]]
    )
    (kept,) = call(
        functools.partial(add_kernel, range(1), (1,)),
        "kept",
        [product],
        [beside, own, parts[0]],
        work=64 * rows * own.size,
    )
    shares = {0: kept, **{k: sent[k - 1] for k in range(1, top)}}
    distance = 1
    while distance < top:
        shares = {
            k: shares[k].astype(F32)
            + swap(shares[k ^ distance].astype(BF16), "mp", mp, distance).astype(F32)
            for k in shares
            if not k & distance
        }
        distance *= 2
    return shares[0].astype(node_vectors.dtype)


def solution(mesh):
    return jax.shard_map(
        lambda *arrays: per_device(mesh, *arrays),
        mesh=mesh,
        in_specs=(
            P(("groups", "seq"), "mp"),
            P(),
            P(None, "mp"),
            P(None, "mp"),
            P(None, "mp"),
            P("mp"),
            P("mp", None),
        ),
        out_specs=P(("groups", "seq"), "mp"),
        check_vma=False,
    )
```

```python
import functools
import math

import jax
import jax.numpy as jnp
from jax import lax
from jax.experimental import pallas as pl
from jax.experimental.pallas import tpu as pltpu
from jax.sharding import PartitionSpec as P

F32, BF16 = jnp.float32, jnp.bfloat16
VMEM = pl.BlockSpec(memory_space=pltpu.VMEM)
HBM = pl.BlockSpec(memory_space=pltpu.HBM)
LANES = 128


def call(kernel, name, out_shape, operands, work=0, limit=16, specs=None, scratch=()):
    return pl.pallas_call(
        kernel,
        out_shape=out_shape,
        in_specs=specs or [VMEM] * len(operands),
        out_specs=[VMEM] * len(out_shape),
        scratch_shapes=scratch,
        compiler_params=pltpu.CompilerParams(vmem_limit_bytes=limit << 20),
        cost_estimate=pl.CostEstimate(flops=work, bytes_accessed=work // 64, transcendentals=0),
        name=name,
    )(*operands)


def swap(block, axis, count, distance):
    return lax.ppermute(block, axis, [(i, i ^ distance) for i in range(count)])


def after(value, *others):
    return lax.optimization_barrier((value, *others))[0]


def prepare_kernel(mp, step, gain_ref, probe_ref, lookup_ref, content_ref, exit_ref, *refs):
    weight_refs, (sums_ref, gain_out_ref, own_ref, far_ref) = refs[:3], refs[3:7]
    rows_ref, sems, gain_sem, exit_sems = refs[7:]
    me = lax.axis_index("mp")
    depth, cols = probe_ref.shape
    parts = sems.shape[0]
    chunk = depth // parts
    gain_copy = pltpu.make_async_copy(gain_ref, gain_out_ref, gain_sem)
    gain_copy.start()
    copies = []
    for c in range(parts):
        rows = pl.ds(c * chunk, chunk)
        copies.append([])
        for i, ref in enumerate((probe_ref, lookup_ref, content_ref)):
            copy = pltpu.make_async_copy(ref.at[rows, :], weight_refs[i].at[rows, :], sems.at[c, i])
            copy.start()
            copies[c].append(copy)
    half, _, width = own_ref.shape
    exits = []
    for k in range(mp):
        to = own_ref.at[k] if k < half else far_ref.at[k - half]
        owner = me ^ k if k < half else me ^ step ^ (k - half)
        columns = pl.ds(pl.multiple_of(owner * width, width), width)
        exits.append(pltpu.make_async_copy(exit_ref.at[:, columns], to, exit_sems.at[k]))
        exits[k].start()
    gain_copy.wait()
    gain = gain_out_ref[...]
    high = gain.astype(BF16)
    rows_ref[...] = jnp.zeros_like(rows_ref)
    rows_ref[0:1, :] = high
    rows_ref[16:17, :] = (gain - high.astype(F32)).astype(BF16)
    for c in range(parts):
        for copy in copies[c]:
            copy.wait()
        span = pl.ds(c * chunk, chunk)
        for i, ref in enumerate(weight_refs):
            part = jnp.dot(rows_ref[:, span], ref[span, :], preferred_element_type=F32)
            part = part[0:8, :] + part[16:24, :]
            if c == 0:
                sums_ref[i] = part
            else:
                sums_ref[i] += part
    for copy in exits:
        copy.wait()


def prepare(mp, step, gain, probe, lookup, content, exit_matrix):
    depth, cols = probe.shape
    deep, wide = exit_matrix.shape
    parts = 4
    stack = pltpu.VMEM((mp // 2, deep, wide // mp), BF16)
    probe, lookup, content, sums, gain, own, far = call(
        functools.partial(prepare_kernel, mp, step),
        "prepare",
        [pltpu.VMEM((depth, cols), BF16)] * 3
        + [pltpu.VMEM((3, 8, cols), F32), pltpu.VMEM((1, depth), F32), stack, stack],
        [
            pltpu.with_memory_space_constraint(w, pltpu.HBM)
            for w in (gain[None, :], probe, lookup, content, exit_matrix)
        ],
        work=48 * depth * cols,
        specs=[HBM] * 5,
        scratch=[
            pltpu.VMEM((32, depth), BF16),
            pltpu.SemaphoreType.DMA((parts, 3)),
            pltpu.SemaphoreType.DMA,
            pltpu.SemaphoreType.DMA((mp,)),
        ],
    )
    return (probe, lookup, content), sums, gain, own, far


def matmul(blocks, places, weight_ref):
    me = lax.axis_index("mp")
    total = None
    for k, block in zip(places, blocks):
        depth = block.shape[1]
        w = weight_ref[pl.ds(pl.multiple_of((me ^ k) * depth, depth), depth), :]
        part = jnp.dot(block[...], w, preferred_element_type=F32)
        total = part if total is None else total + part
    return total


def take_in(blocks, places, shift, gain_ref, weight_refs):
    me = lax.axis_index("mp")
    one, two, scaled = 0.0, 0.0, []
    for k, block in zip(places, blocks):
        width = block.shape[1]
        gain = gain_ref[0:1, pl.ds(pl.multiple_of((me ^ k) * width, width), width)]
        moved = block[...].astype(F32) - shift
        scaled.append((moved * gain).astype(BF16))
        one += jnp.sum(moved, axis=1, keepdims=True)
        two += jnp.sum(moved * moved, axis=1, keepdims=True)
    return one, two, [matmul(scaled, places, ref) for ref in weight_refs]


def early_kernel(places, *refs):
    count = len(places)
    blocks = refs[:count]
    weight_refs, (gain_ref, factor_ref, stats_ref), product_refs, (factor_out_ref,) = (
        refs[count : count + 3],
        refs[count + 3 : count + 6],
        refs[count + 6 : count + 9],
        refs[count + 9 :],
    )
    factor_out_ref[...] = factor_ref[...]
    shift = jnp.mean(blocks[0][...].astype(F32), axis=1, keepdims=True)
    one, two, products = take_in(blocks, places, shift, gain_ref, weight_refs)
    for ref, product in zip(product_refs, products):
        ref[...] = product
    for i, value in enumerate((shift, one, two)):
        stats_ref[i] = jnp.broadcast_to(value, stats_ref.shape[1:])


def parity():
    return lax.rem(lax.axis_index("seq"), 2)


def late_kernel(places, depth, *refs):
    count = len(places)
    blocks, refs = refs[:count], refs[count:]
    weight_refs, (gain_ref, sums_ref, stats_ref, factor_ref), product_refs = refs[:3], refs[3:7], refs[7:10]
    queries_ref, mine_ref, other_ref, bundle_ref = refs[10:]
    one, two, products = take_in(blocks, places, stats_ref[0, :, 0:1], gain_ref, weight_refs)
    offset = (one + stats_ref[1, :, 0:1]) / depth
    scale = lax.rsqrt((two + stats_ref[2, :, 0:1]) / depth - offset * offset + 1e-05)
    first = parity() == 0
    parts = []
    for i, (product, ref) in enumerate(zip(products, product_refs)):
        product = product + ref[...]
        product = scale * (product - offset * sums_ref[i, 0:1, :])
        if i == 0:
            product = product * factor_ref[...]
        half = product.shape[1] // 2
        low, high = product[:, :half], product[:, half:]
        parts.append([jnp.where(first, *v).astype(BF16) for v in ((low, high), (high, low))])
    for i in range(2):
        for h in range(half // LANES):
            span = slice(h * LANES, (h + 1) * LANES)
            to = pl.ds((2 * h + i) * LANES, LANES)
            mine_ref[:, to] = parts[i + 1][0][:, span]
            other_ref[:, to] = parts[i + 1][1][:, span]
            bundle_ref[:, to] = parts[i + 1][1][:, span]
    queries_ref[...] = parts[0][0]
    bundle_ref[:, pl.ds(2 * half, half)] = parts[0][1]


def project(blocks, places, weights, sums, gain, factor):
    rows, width = blocks[0].shape
    cols = weights[0].shape[1]
    count = len(blocks)
    product = pltpu.VMEM((rows, cols), F32)
    stats, *products, factor = call(
        functools.partial(early_kernel, places[:-1]),
        "early",
        [pltpu.VMEM((3, rows, LANES), F32), product, product, product, pltpu.VMEM(factor.shape, F32)],
        [*blocks[:-1], *weights, gain, factor],
        work=16 * rows * weights[0].size,
    )
    pair = pltpu.VMEM((rows, cols), BF16)
    return call(
        functools.partial(late_kernel, places[-1:], count * width),
        "late",
        [pltpu.VMEM((rows, cols // 2), BF16), pair, pair, pltpu.VMEM((rows, 3 * cols // 2), BF16)],
        [blocks[-1], *weights, gain, sums, stats, factor, *products],
    )


def merge_kernel(*refs):
    rows = refs[0].shape[0]
    for i, ref in enumerate(refs[:-1]):
        refs[-1][pl.ds(i * rows, rows), :] = ref[...]


def attend_kernel(count, mine_ref, bundle_ref, *refs):
    blocks, out_refs = refs[:count], refs[count:]
    half = mine_ref.shape[1]
    rows = mine_ref.shape[0]
    for h in range(half // LANES):
        q = jnp.concatenate(
            [mine_ref[:, pl.ds(h * LANES, LANES)], bundle_ref[:, pl.ds(2 * half + h * LANES, LANES)]], axis=0
        )
        scores = [
            lax.dot_general(
                q, b[:, pl.ds(2 * h * LANES, LANES)], (((1,), (1,)), ((), ())), preferred_element_type=F32
            )
            for b in blocks
        ]
        top = functools.reduce(jnp.maximum, [jnp.max(s, axis=1, keepdims=True) for s in scores])
        weights = [jnp.exp2(s - top) for s in scores]
        weighted = sum(
            jnp.dot(
                w.astype(BF16), b[:, pl.ds((2 * h + 1) * LANES, LANES)], preferred_element_type=F32
            )
            for w, b in zip(weights, blocks)
        )
        total = sum(jnp.sum(w, axis=1, keepdims=True) for w in weights)
        out = (weighted / total).astype(BF16)
        for i, ref in enumerate(out_refs):
            ref[:, pl.ds(h * LANES, LANES)] = out[i * rows : (i + 1) * rows, :]


def attend(queries, bundle, blocks):
    rows, wide = blocks[0].shape
    (merged,) = call(
        merge_kernel,
        "merge",
        [pltpu.VMEM((len(blocks) * rows, wide), BF16)],
        blocks,
        work=30000 * rows * wide * len(blocks),
    )
    size = merged.shape[0]
    return call(
        functools.partial(attend_kernel, 2),
        "attend",
        [pltpu.VMEM(queries.shape, BF16)] * 2,
        [queries, bundle, bundle, merged],
        limit=56 if size > 2048 else 16,
    )


def own_kernel(x_ref, mixed_ref, exit_ref, *out_refs):
    deep = mixed_ref.shape[1]
    rows = pl.ds(pl.multiple_of(parity() * deep, deep), deep)
    for k, ref in enumerate(out_refs):
        part = jnp.dot(mixed_ref[...], exit_ref[k, rows, :], preferred_element_type=F32)
        ref[...] = part + x_ref[...].astype(F32) if k == 0 else part


def add_kernel(which, flips, *refs):
    count, values = len(which), len(flips)
    for i, k in enumerate(which):
        total = refs[2 * values + i][...]
        for j, flip in enumerate(flips):
            deep = refs[j].shape[1]
            at = 1 - parity() if flip else parity()
            rows = pl.ds(pl.multiple_of(at * deep, deep), deep)
            total += jnp.dot(refs[j][...], refs[values + j][k, rows, :], preferred_element_type=F32)
        out_ref = refs[2 * values + count + i]
        out_ref[...] = total.astype(out_ref.dtype)


def per_device(mesh, node_vectors, gain, probe, lookup, content, softness, exit_matrix):
    mp, seq = mesh.shape["mp"], mesh.shape["seq"]
    heads = softness.shape[0]
    cols = probe.shape[1]
    span = cols // heads
    top = mp // 2
    step = top | 1
    factor = jnp.repeat(softness * (math.log2(math.e) / math.sqrt(span)), span)[None, :]

    weights, sums, gains, own, far = prepare(mp, step, gain, probe, lookup, content, exit_matrix)
    blocks, distance = {0: node_vectors}, step
    while distance:
        new = {k ^ distance: swap(b, "mp", mp, distance) for k, b in blocks.items()}
        if distance == step:
            new, sums = lax.optimization_barrier((new, sums))
        blocks.update(new)
        distance = top // 2 if distance == step else distance // 2
    places = sorted(blocks, key=lambda k: (k & top, bool(k & top) and k ^ step))
    queries, mine, other, bundle = project(
        [blocks[k] for k in places], places, weights, sums, gains, factor
    )
    theirs = swap(far, "mp", mp, step)

    found = {0: mine}
    for k in sorted(range(1, seq), key=lambda k: (k == 1, k)):
        found[k] = swap(bundle if k == 1 else other if k % 2 else mine, "seq", seq, k)
    mixed, mixed_beside = attend(queries, found[1], [found[k] for k in range(seq) if k != 1])

    rows, width = node_vectors.shape
    product, half = pltpu.VMEM((rows, width), F32), pltpu.VMEM((rows, width), BF16)
    both = ("seq", "mp")
    across = swap(mixed, both, seq * mp, step)
    beside = swap(mixed_beside, both, seq * mp, mp)
    corner = swap(mixed_beside, both, seq * mp, mp + step)
    parts = call(
        own_kernel, "own", [product] * top, [node_vectors, mixed, own], work=1 * rows * own.size
    )
    parts = call(
        functools.partial(add_kernel, range(top), (0, 1)),
        "crossed",
        [product] * top,
        [across, corner, theirs, theirs, *parts],
        work=64 * rows * own.size,
    )
    sent = call(
        functools.partial(add_kernel, range(1, top), (1,)), "sent", [half] * (top - 1), [beside, own, *parts[1:]]
    )
    (kept,) = call(
        functools.partial(add_kernel, range(1), (1,)),
        "kept",
        [product],
        [beside, own, parts[0]],
        work=64 * rows * own.size,
    )
    shares = {0: kept, **{k: sent[k - 1] for k in range(1, top)}}
    distance = 1
    while distance < top:
        shares = {
            k: shares[k].astype(F32)
            + swap(shares[k ^ distance].astype(BF16), "mp", mp, distance).astype(F32)
            for k in shares
            if not k & distance
        }
        distance *= 2
    return shares[0].astype(node_vectors.dtype)


def solution(mesh):
    return jax.shard_map(
        lambda *arrays: per_device(mesh, *arrays),
        mesh=mesh,
        in_specs=(
            P(("groups", "seq"), "mp"),
            P(),
            P(None, "mp"),
            P(None, "mp"),
            P(None, "mp"),
            P("mp"),
            P("mp", None),
        ),
        out_specs=P(("groups", "seq"), "mp"),
        check_vma=False,
    )
```

```python
import functools
import math

import jax
import jax.numpy as jnp
from jax import lax
from jax.experimental import pallas as pl
from jax.experimental.pallas import tpu as pltpu
from jax.sharding import PartitionSpec as P

F32, BF16 = jnp.float32, jnp.bfloat16
VMEM = pl.BlockSpec(memory_space=pltpu.VMEM)
HBM = pl.BlockSpec(memory_space=pltpu.HBM)
LANES = 128


def call(kernel, name, out_shape, operands, work=0, limit=16, specs=None, scratch=()):
    return pl.pallas_call(
        kernel,
        out_shape=out_shape,
        in_specs=specs or [VMEM] * len(operands),
        out_specs=[VMEM] * len(out_shape),
        scratch_shapes=scratch,
        compiler_params=pltpu.CompilerParams(vmem_limit_bytes=limit << 20),
        cost_estimate=pl.CostEstimate(flops=work, bytes_accessed=work // 64, transcendentals=0),
        name=name,
    )(*operands)


def swap(block, axis, count, distance):
    return lax.ppermute(block, axis, [(i, i ^ distance) for i in range(count)])


def after(value, *others):
    return lax.optimization_barrier((value, *others))[0]


def prepare_kernel(mp, step, gain_ref, probe_ref, lookup_ref, content_ref, exit_ref, *refs):
    weight_refs, (sums_ref, gain_out_ref, own_ref, far_ref) = refs[:3], refs[3:7]
    rows_ref, sems, gain_sem, exit_sems = refs[7:]
    me = lax.axis_index("mp")
    depth, cols = probe_ref.shape
    parts = sems.shape[0]
    chunk = depth // parts
    gain_copy = pltpu.make_async_copy(gain_ref, gain_out_ref, gain_sem)
    gain_copy.start()
    copies = []
    for c in range(parts):
        rows = pl.ds(c * chunk, chunk)
        copies.append([])
        for i, ref in enumerate((probe_ref, lookup_ref, content_ref)):
            copy = pltpu.make_async_copy(ref.at[rows, :], weight_refs[i].at[rows, :], sems.at[c, i])
            copy.start()
            copies[c].append(copy)
    half, _, width = own_ref.shape
    exits = []
    for k in range(mp):
        to = own_ref.at[k] if k < half else far_ref.at[k - half]
        owner = me ^ k if k < half else me ^ step ^ (k - half)
        columns = pl.ds(pl.multiple_of(owner * width, width), width)
        exits.append(pltpu.make_async_copy(exit_ref.at[:, columns], to, exit_sems.at[k]))
        exits[k].start()
    gain_copy.wait()
    gain = gain_out_ref[...]
    high = gain.astype(BF16)
    rows_ref[...] = jnp.zeros_like(rows_ref)
    rows_ref[0:1, :] = high
    rows_ref[16:17, :] = (gain - high.astype(F32)).astype(BF16)
    for c in range(parts):
        for copy in copies[c]:
            copy.wait()
        span = pl.ds(c * chunk, chunk)
        for i, ref in enumerate(weight_refs):
            part = jnp.dot(rows_ref[:, span], ref[span, :], preferred_element_type=F32)
            part = part[0:8, :] + part[16:24, :]
            if c == 0:
                sums_ref[i] = part
            else:
                sums_ref[i] += part
    for copy in exits:
        copy.wait()


def prepare(mp, step, gain, probe, lookup, content, exit_matrix):
    depth, cols = probe.shape
    deep, wide = exit_matrix.shape
    parts = 4
    stack = pltpu.VMEM((mp // 2, deep, wide // mp), BF16)
    probe, lookup, content, sums, gain, own, far = call(
        functools.partial(prepare_kernel, mp, step),
        "prepare",
        [pltpu.VMEM((depth, cols), BF16)] * 3
        + [pltpu.VMEM((3, 8, cols), F32), pltpu.VMEM((1, depth), F32), stack, stack],
        [
            pltpu.with_memory_space_constraint(w, pltpu.HBM)
            for w in (gain[None, :], probe, lookup, content, exit_matrix)
        ],
        work=48 * depth * cols,
        specs=[HBM] * 5,
        scratch=[
            pltpu.VMEM((32, depth), BF16),
            pltpu.SemaphoreType.DMA((parts, 3)),
            pltpu.SemaphoreType.DMA,
            pltpu.SemaphoreType.DMA((mp,)),
        ],
    )
    return (probe, lookup, content), sums, gain, own, far


def matmul(blocks, places, weight_ref):
    me = lax.axis_index("mp")
    total = None
    for k, block in zip(places, blocks):
        depth = block.shape[1]
        w = weight_ref[pl.ds(pl.multiple_of((me ^ k) * depth, depth), depth), :]
        part = jnp.dot(block[...], w, preferred_element_type=F32)
        total = part if total is None else total + part
    return total


def take_in(blocks, places, shift, gain_ref, weight_refs):
    me = lax.axis_index("mp")
    one, two, scaled = 0.0, 0.0, []
    for k, block in zip(places, blocks):
        width = block.shape[1]
        gain = gain_ref[0:1, pl.ds(pl.multiple_of((me ^ k) * width, width), width)]
        moved = block[...].astype(F32) - shift
        scaled.append((moved * gain).astype(BF16))
        one += jnp.sum(moved, axis=1, keepdims=True)
        two += jnp.sum(moved * moved, axis=1, keepdims=True)
    return one, two, [matmul(scaled, places, ref) for ref in weight_refs]


def early_kernel(places, *refs):
    count = len(places)
    blocks = refs[:count]
    weight_refs, (gain_ref, factor_ref, stats_ref), product_refs, (factor_out_ref,) = (
        refs[count : count + 3],
        refs[count + 3 : count + 6],
        refs[count + 6 : count + 9],
        refs[count + 9 :],
    )
    factor_out_ref[...] = factor_ref[...]
    shift = jnp.mean(blocks[0][...].astype(F32), axis=1, keepdims=True)
    one, two, products = take_in(blocks, places, shift, gain_ref, weight_refs)
    for ref, product in zip(product_refs, products):
        ref[...] = product
    for i, value in enumerate((shift, one, two)):
        stats_ref[i] = jnp.broadcast_to(value, stats_ref.shape[1:])


def parity():
    return lax.rem(lax.axis_index("seq"), 2)


def late_kernel(places, depth, *refs):
    count = len(places)
    blocks, refs = refs[:count], refs[count:]
    weight_refs, (gain_ref, sums_ref, stats_ref, factor_ref), product_refs = refs[:3], refs[3:7], refs[7:10]
    queries_ref, mine_ref, other_ref, bundle_ref = refs[10:]
    one, two, products = take_in(blocks, places, stats_ref[0, :, 0:1], gain_ref, weight_refs)
    offset = (one + stats_ref[1, :, 0:1]) / depth
    scale = lax.rsqrt((two + stats_ref[2, :, 0:1]) / depth - offset * offset + 1e-05)
    first = parity() == 0
    parts = []
    for i, (product, ref) in enumerate(zip(products, product_refs)):
        product = product + ref[...]
        product = scale * (product - offset * sums_ref[i, 0:1, :])
        if i == 0:
            product = product * factor_ref[...]
        half = product.shape[1] // 2
        low, high = product[:, :half], product[:, half:]
        parts.append([jnp.where(first, *v).astype(BF16) for v in ((low, high), (high, low))])
    for i in range(2):
        for h in range(half // LANES):
            span = slice(h * LANES, (h + 1) * LANES)
            to = pl.ds((2 * h + i) * LANES, LANES)
            mine_ref[:, to] = parts[i + 1][0][:, span]
            other_ref[:, to] = parts[i + 1][1][:, span]
            bundle_ref[:, to] = parts[i + 1][1][:, span]
    queries_ref[...] = parts[0][0]
    bundle_ref[:, pl.ds(2 * half, half)] = parts[0][1]


def project(blocks, places, weights, sums, gain, factor):
    rows, width = blocks[0].shape
    cols = weights[0].shape[1]
    count = len(blocks)
    product = pltpu.VMEM((rows, cols), F32)
    stats, *products, factor = call(
        functools.partial(early_kernel, places[:-1]),
        "early",
        [pltpu.VMEM((3, rows, LANES), F32), product, product, product, pltpu.VMEM(factor.shape, F32)],
        [*blocks[:-1], *weights, gain, factor],
        work=16 * rows * weights[0].size,
    )
    pair = pltpu.VMEM((rows, cols), BF16)
    return call(
        functools.partial(late_kernel, places[-1:], count * width),
        "late",
        [pltpu.VMEM((rows, cols // 2), BF16), pair, pair, pltpu.VMEM((rows, 3 * cols // 2), BF16)],
        [blocks[-1], *weights, gain, sums, stats, factor, *products],
    )


def merge_kernel(*refs):
    rows = refs[0].shape[0]
    for i, ref in enumerate(refs[:-1]):
        refs[-1][pl.ds(i * rows, rows), :] = ref[...]


def attend_kernel(count, mine_ref, bundle_ref, *refs):
    blocks, out_refs = refs[:count], refs[count:]
    half = mine_ref.shape[1]
    rows = mine_ref.shape[0]
    for h in range(half // LANES):
        q = jnp.concatenate(
            [mine_ref[:, pl.ds(h * LANES, LANES)], bundle_ref[:, pl.ds(2 * half + h * LANES, LANES)]], axis=0
        )
        scores = [
            lax.dot_general(
                q, b[:, pl.ds(2 * h * LANES, LANES)], (((1,), (1,)), ((), ())), preferred_element_type=F32
            )
            for b in blocks
        ]
        top = functools.reduce(jnp.maximum, [jnp.max(s, axis=1, keepdims=True) for s in scores])
        weights = [jnp.exp2(s - top) for s in scores]
        weighted = sum(
            jnp.dot(
                w.astype(BF16), b[:, pl.ds((2 * h + 1) * LANES, LANES)], preferred_element_type=F32
            )
            for w, b in zip(weights, blocks)
        )
        total = sum(jnp.sum(w, axis=1, keepdims=True) for w in weights)
        out = (weighted / total).astype(BF16)
        for i, ref in enumerate(out_refs):
            ref[:, pl.ds(h * LANES, LANES)] = out[i * rows : (i + 1) * rows, :]


def attend(queries, bundle, blocks):
    rows, wide = blocks[0].shape
    (merged,) = call(
        merge_kernel,
        "merge",
        [pltpu.VMEM((len(blocks) * rows, wide), BF16)],
        blocks,
        work=30000 * rows * wide * len(blocks),
    )
    size = merged.shape[0]
    return call(
        functools.partial(attend_kernel, 2),
        "attend",
        [pltpu.VMEM(queries.shape, BF16)] * 2,
        [queries, bundle, bundle, merged],
        limit=56 if size > 2048 else 16,
    )


def own_kernel(x_ref, mixed_ref, exit_ref, *out_refs):
    deep = mixed_ref.shape[1]
    rows = pl.ds(pl.multiple_of(parity() * deep, deep), deep)
    for k, ref in enumerate(out_refs):
        part = jnp.dot(mixed_ref[...], exit_ref[k, rows, :], preferred_element_type=F32)
        ref[...] = part + x_ref[...].astype(F32) if k == 0 else part


def add_kernel(which, flips, *refs):
    count, values = len(which), len(flips)
    for i, k in enumerate(which):
        total = refs[2 * values + i][...]
        for j, flip in enumerate(flips):
            deep = refs[j].shape[1]
            at = 1 - parity() if flip else parity()
            rows = pl.ds(pl.multiple_of(at * deep, deep), deep)
            total += jnp.dot(refs[j][...], refs[values + j][k, rows, :], preferred_element_type=F32)
        out_ref = refs[2 * values + count + i]
        out_ref[...] = total.astype(out_ref.dtype)


def per_device(mesh, node_vectors, gain, probe, lookup, content, softness, exit_matrix):
    mp, seq = mesh.shape["mp"], mesh.shape["seq"]
    heads = softness.shape[0]
    cols = probe.shape[1]
    span = cols // heads
    top = mp // 2
    step = top | 1
    factor = jnp.repeat(softness * (math.log2(math.e) / math.sqrt(span)), span)[None, :]

    weights, sums, gains, own, far = prepare(mp, step, gain, probe, lookup, content, exit_matrix)
    blocks, distance = {0: node_vectors}, top
    while distance:
        new = {k ^ distance: swap(b, "mp", mp, distance) for k, b in blocks.items()}
        if distance == top:
            new, sums = lax.optimization_barrier((new, sums))
        blocks.update(new)
        distance //= 2
    places = range(mp)
    queries, mine, other, bundle = project(
        [blocks[k] for k in places], places, weights, sums, gains, factor
    )
    theirs = swap(far, "mp", mp, step)

    found = {0: mine}
    for k in sorted(range(1, seq), key=lambda k: (k == 1, k)):
        found[k] = swap(bundle if k == 1 else other if k % 2 else mine, "seq", seq, k)
    mixed, mixed_beside = attend(queries, found[1], [found[k] for k in range(seq) if k != 1])

    rows, width = node_vectors.shape
    product, half = pltpu.VMEM((rows, width), F32), pltpu.VMEM((rows, width), BF16)
    both = ("seq", "mp")
    across = swap(mixed, both, seq * mp, step)
    beside = swap(mixed_beside, both, seq * mp, mp)
    corner = swap(mixed_beside, both, seq * mp, mp + step)
    parts = call(
        own_kernel, "own", [product] * top, [node_vectors, mixed, own], work=1 * rows * own.size
    )
    parts = call(
        functools.partial(add_kernel, range(top), (0, 1)),
        "crossed",
        [product] * top,
        [across, corner, theirs, theirs, *parts],
        work=64 * rows * own.size,
    )
    sent = call(
        functools.partial(add_kernel, range(1, top), (1,)), "sent", [half] * (top - 1), [beside, own, *parts[1:]]
    )
    (kept,) = call(
        functools.partial(add_kernel, range(1), (1,)),
        "kept",
        [product],
        [beside, own, parts[0]],
        work=64 * rows * own.size,
    )
    shares = {0: kept, **{k: sent[k - 1] for k in range(1, top)}}
    distance = 1
    while distance < top:
        shares = {
            k: shares[k].astype(F32)
            + swap(shares[k ^ distance].astype(BF16), "mp", mp, distance).astype(F32)
            for k in shares
            if not k & distance
        }
        distance *= 2
    return shares[0].astype(node_vectors.dtype)


def solution(mesh):
    return jax.shard_map(
        lambda *arrays: per_device(mesh, *arrays),
        mesh=mesh,
        in_specs=(
            P(("groups", "seq"), "mp"),
            P(),
            P(None, "mp"),
            P(None, "mp"),
            P(None, "mp"),
            P("mp"),
            P("mp", None),
        ),
        out_specs=P(("groups", "seq"), "mp"),
        check_vma=False,
    )
```

```python
import functools
import math

import jax
import jax.numpy as jnp
from jax import lax
from jax.experimental import pallas as pl
from jax.experimental.pallas import tpu as pltpu
from jax.sharding import PartitionSpec as P

F32, BF16 = jnp.float32, jnp.bfloat16
VMEM = pl.BlockSpec(memory_space=pltpu.VMEM)
HBM = pl.BlockSpec(memory_space=pltpu.HBM)
LANES = 128


def call(kernel, name, out_shape, operands, work=0, limit=16, specs=None, scratch=()):
    return pl.pallas_call(
        kernel,
        out_shape=out_shape,
        in_specs=specs or [VMEM] * len(operands),
        out_specs=[VMEM] * len(out_shape),
        scratch_shapes=scratch,
        compiler_params=pltpu.CompilerParams(vmem_limit_bytes=limit << 20),
        cost_estimate=pl.CostEstimate(flops=work, bytes_accessed=work // 64, transcendentals=0),
        name=name,
    )(*operands)


def swap(block, axis, count, distance):
    return lax.ppermute(block, axis, [(i, i ^ distance) for i in range(count)])


def after(value, *others):
    return lax.optimization_barrier((value, *others))[0]


def prepare_kernel(mp, step, gain_ref, probe_ref, lookup_ref, content_ref, exit_ref, *refs):
    weight_refs, (sums_ref, gain_out_ref, own_ref, far_ref) = refs[:3], refs[3:7]
    rows_ref, sems, gain_sem, exit_sems = refs[7:]
    me = lax.axis_index("mp")
    depth, cols = probe_ref.shape
    parts = sems.shape[0]
    chunk = depth // parts
    gain_copy = pltpu.make_async_copy(gain_ref, gain_out_ref, gain_sem)
    gain_copy.start()
    copies = []
    for c in range(parts):
        rows = pl.ds(c * chunk, chunk)
        copies.append([])
        for i, ref in enumerate((probe_ref, lookup_ref, content_ref)):
            copy = pltpu.make_async_copy(ref.at[rows, :], weight_refs[i].at[rows, :], sems.at[c, i])
            copy.start()
            copies[c].append(copy)
    half, _, width = own_ref.shape
    exits = []
    for k in range(mp):
        to = own_ref.at[k] if k < half else far_ref.at[k - half]
        owner = me ^ k if k < half else me ^ step ^ (k - half)
        columns = pl.ds(pl.multiple_of(owner * width, width), width)
        exits.append(pltpu.make_async_copy(exit_ref.at[:, columns], to, exit_sems.at[k]))
        exits[k].start()
    gain_copy.wait()
    gain = gain_out_ref[...]
    high = gain.astype(BF16)
    rows_ref[...] = jnp.zeros_like(rows_ref)
    rows_ref[0:1, :] = high
    rows_ref[16:17, :] = (gain - high.astype(F32)).astype(BF16)
    for c in range(parts):
        for copy in copies[c]:
            copy.wait()
        span = pl.ds(c * chunk, chunk)
        for i, ref in enumerate(weight_refs):
            part = jnp.dot(rows_ref[:, span], ref[span, :], preferred_element_type=F32)
            part = part[0:8, :] + part[16:24, :]
            if c == 0:
                sums_ref[i] = part
            else:
                sums_ref[i] += part
    for copy in exits:
        copy.wait()


def prepare(mp, step, gain, probe, lookup, content, exit_matrix):
    depth, cols = probe.shape
    deep, wide = exit_matrix.shape
    parts = 4
    stack = pltpu.VMEM((mp // 2, deep, wide // mp), BF16)
    probe, lookup, content, sums, gain, own, far = call(
        functools.partial(prepare_kernel, mp, step),
        "prepare",
        [pltpu.VMEM((depth, cols), BF16)] * 3
        + [pltpu.VMEM((3, 8, cols), F32), pltpu.VMEM((1, depth), F32), stack, stack],
        [
            pltpu.with_memory_space_constraint(w, pltpu.HBM)
            for w in (gain[None, :], probe, lookup, content, exit_matrix)
        ],
        work=48 * depth * cols,
        specs=[HBM] * 5,
        scratch=[
            pltpu.VMEM((32, depth), BF16),
            pltpu.SemaphoreType.DMA((parts, 3)),
            pltpu.SemaphoreType.DMA,
            pltpu.SemaphoreType.DMA((mp,)),
        ],
    )
    return (probe, lookup, content), sums, gain, own, far


def matmul(blocks, places, weight_ref):
    me = lax.axis_index("mp")
    total = None
    for k, block in zip(places, blocks):
        depth = block.shape[1]
        w = weight_ref[pl.ds(pl.multiple_of((me ^ k) * depth, depth), depth), :]
        part = jnp.dot(block[...], w, preferred_element_type=F32)
        total = part if total is None else total + part
    return total


def take_in(blocks, places, shift, gain_ref, weight_refs):
    me = lax.axis_index("mp")
    one, two, scaled = 0.0, 0.0, []
    for k, block in zip(places, blocks):
        width = block.shape[1]
        gain = gain_ref[0:1, pl.ds(pl.multiple_of((me ^ k) * width, width), width)]
        moved = block[...].astype(F32) - shift
        scaled.append((moved * gain).astype(BF16))
        one += jnp.sum(moved, axis=1, keepdims=True)
        two += jnp.sum(moved * moved, axis=1, keepdims=True)
    return one, two, [matmul(scaled, places, ref) for ref in weight_refs]


def early_kernel(places, *refs):
    count = len(places)
    blocks = refs[:count]
    weight_refs, (gain_ref, factor_ref, stats_ref), product_refs, (factor_out_ref,) = (
        refs[count : count + 3],
        refs[count + 3 : count + 6],
        refs[count + 6 : count + 9],
        refs[count + 9 :],
    )
    factor_out_ref[...] = factor_ref[...]
    shift = jnp.mean(blocks[0][...].astype(F32), axis=1, keepdims=True)
    one, two, products = take_in(blocks, places, shift, gain_ref, weight_refs)
    for ref, product in zip(product_refs, products):
        ref[...] = product
    for i, value in enumerate((shift, one, two)):
        stats_ref[i] = jnp.broadcast_to(value, stats_ref.shape[1:])


def parity():
    return lax.rem(lax.axis_index("seq"), 2)


def late_kernel(places, depth, *refs):
    count = len(places)
    blocks, refs = refs[:count], refs[count:]
    weight_refs, (gain_ref, sums_ref, stats_ref, factor_ref), product_refs = refs[:3], refs[3:7], refs[7:10]
    queries_ref, mine_ref, other_ref, bundle_ref = refs[10:]
    one, two, products = take_in(blocks, places, stats_ref[0, :, 0:1], gain_ref, weight_refs)
    offset = (one + stats_ref[1, :, 0:1]) / depth
    scale = lax.rsqrt((two + stats_ref[2, :, 0:1]) / depth - offset * offset + 1e-05)
    first = parity() == 0
    parts = []
    for i, (product, ref) in enumerate(zip(products, product_refs)):
        product = product + ref[...]
        product = scale * (product - offset * sums_ref[i, 0:1, :])
        if i == 0:
            product = product * factor_ref[...]
        half = product.shape[1] // 2
        low, high = product[:, :half], product[:, half:]
        parts.append([jnp.where(first, *v).astype(BF16) for v in ((low, high), (high, low))])
    for i in range(2):
        for h in range(half // LANES):
            span = slice(h * LANES, (h + 1) * LANES)
            to = pl.ds((2 * h + i) * LANES, LANES)
            mine_ref[:, to] = parts[i + 1][0][:, span]
            other_ref[:, to] = parts[i + 1][1][:, span]
            bundle_ref[:, to] = parts[i + 1][1][:, span]
    queries_ref[...] = parts[0][0]
    bundle_ref[:, pl.ds(2 * half, half)] = parts[0][1]


def project(blocks, places, weights, sums, gain, factor):
    rows, width = blocks[0].shape
    cols = weights[0].shape[1]
    count = len(blocks)
    product = pltpu.VMEM((rows, cols), F32)
    stats, *products, factor = call(
        functools.partial(early_kernel, places[:-1]),
        "early",
        [pltpu.VMEM((3, rows, LANES), F32), product, product, product, pltpu.VMEM(factor.shape, F32)],
        [*blocks[:-1], *weights, gain, factor],
        work=16 * rows * weights[0].size,
    )
    pair = pltpu.VMEM((rows, cols), BF16)
    return call(
        functools.partial(late_kernel, places[-1:], count * width),
        "late",
        [pltpu.VMEM((rows, cols // 2), BF16), pair, pair, pltpu.VMEM((rows, 3 * cols // 2), BF16)],
        [blocks[-1], *weights, gain, sums, stats, factor, *products],
    )


def merge_kernel(*refs):
    rows = refs[0].shape[0]
    for i, ref in enumerate(refs[:-1]):
        refs[-1][pl.ds(i * rows, rows), :] = ref[...]


def attend_kernel(count, mine_ref, bundle_ref, *refs):
    blocks, out_refs = refs[:count], refs[count:]
    half = mine_ref.shape[1]
    rows = mine_ref.shape[0]
    for h in range(half // LANES):
        q = jnp.concatenate(
            [mine_ref[:, pl.ds(h * LANES, LANES)], bundle_ref[:, pl.ds(2 * half + h * LANES, LANES)]], axis=0
        )
        scores = [
            lax.dot_general(
                q, b[:, pl.ds(2 * h * LANES, LANES)], (((1,), (1,)), ((), ())), preferred_element_type=F32
            )
            for b in blocks
        ]
        top = functools.reduce(jnp.maximum, [jnp.max(s, axis=1, keepdims=True) for s in scores])
        weights = [jnp.exp2(s - top) for s in scores]
        weighted = sum(
            jnp.dot(
                w.astype(BF16), b[:, pl.ds((2 * h + 1) * LANES, LANES)], preferred_element_type=F32
            )
            for w, b in zip(weights, blocks)
        )
        total = sum(jnp.sum(w, axis=1, keepdims=True) for w in weights)
        out = (weighted / total).astype(BF16)
        for i, ref in enumerate(out_refs):
            ref[:, pl.ds(h * LANES, LANES)] = out[i * rows : (i + 1) * rows, :]


def attend(queries, bundle, blocks):
    rows, wide = blocks[0].shape
    (merged,) = call(
        merge_kernel,
        "merge",
        [pltpu.VMEM((len(blocks) * rows, wide), BF16)],
        blocks,
        work=30000 * rows * wide * len(blocks),
    )
    size = merged.shape[0]
    return call(
        functools.partial(attend_kernel, 2),
        "attend",
        [pltpu.VMEM(queries.shape, BF16)] * 2,
        [queries, bundle, bundle, merged],
        limit=56 if size > 2048 else 16,
    )


def own_kernel(x_ref, mixed_ref, exit_ref, *out_refs):
    deep = mixed_ref.shape[1]
    rows = pl.ds(pl.multiple_of(parity() * deep, deep), deep)
    for k, ref in enumerate(out_refs):
        part = jnp.dot(mixed_ref[...], exit_ref[k, rows, :], preferred_element_type=F32)
        ref[...] = part + x_ref[...].astype(F32) if k == 0 else part


def add_kernel(which, flips, *refs):
    count, values = len(which), len(flips)
    for i, k in enumerate(which):
        total = refs[2 * values + i][...]
        for j, flip in enumerate(flips):
            deep = refs[j].shape[1]
            at = 1 - parity() if flip else parity()
            rows = pl.ds(pl.multiple_of(at * deep, deep), deep)
            total += jnp.dot(refs[j][...], refs[values + j][k, rows, :], preferred_element_type=F32)
        out_ref = refs[2 * values + count + i]
        out_ref[...] = total.astype(out_ref.dtype)


def per_device(mesh, node_vectors, gain, probe, lookup, content, softness, exit_matrix):
    mp, seq = mesh.shape["mp"], mesh.shape["seq"]
    heads = softness.shape[0]
    cols = probe.shape[1]
    span = cols // heads
    top = mp // 2
    step = top | 1
    factor = jnp.repeat(softness * (math.log2(math.e) / math.sqrt(span)), span)[None, :]

    weights, sums, gains, own, far = prepare(mp, step, gain, probe, lookup, content, exit_matrix)
    blocks, distance = {0: node_vectors}, top
    while distance:
        new = {k ^ distance: swap(b, "mp", mp, distance) for k, b in blocks.items()}
        if distance == top:
            new, sums = lax.optimization_barrier((new, sums))
        blocks.update(new)
        distance //= 2
    places = range(mp)
    queries, mine, other, bundle = project(
        [blocks[k] for k in places], places, weights, sums, gains, factor
    )
    theirs = swap(far, "mp", mp, step)

    found = {0: mine}
    for k in sorted(range(1, seq), key=lambda k: (k == 1, k)):
        found[k] = swap(bundle if k == 1 else other if k % 2 else mine, "seq", seq, k)
    mixed, mixed_beside = attend(queries, found[1], [found[k] for k in range(seq) if k != 1])

    rows, width = node_vectors.shape
    product, half = pltpu.VMEM((rows, width), F32), pltpu.VMEM((rows, width), BF16)
    both = ("seq", "mp")
    across = swap(mixed, both, seq * mp, step)
    beside = swap(mixed_beside, both, seq * mp, mp)
    corner = swap(mixed_beside, both, seq * mp, mp + step)
    parts = call(
        own_kernel, "own", [product] * top, [node_vectors, mixed, own], work=1 * rows * own.size
    )
    parts = call(
        functools.partial(add_kernel, range(top), (0,)),
        "crossed",
        [product] * top,
        [across, theirs, *parts],
        work=64 * rows * own.size,
    )
    sent = call(
        functools.partial(add_kernel, range(1, top), (1, 1)),
        "sent",
        [half] * (top - 1),
        [corner, beside, theirs, own, *parts[1:]],
    )
    (kept,) = call(
        functools.partial(add_kernel, range(1), (1, 1)),
        "kept",
        [product],
        [corner, beside, theirs, own, parts[0]],
        work=64 * rows * own.size,
    )
    shares = {0: kept, **{k: sent[k - 1] for k in range(1, top)}}
    distance = 1
    while distance < top:
        shares = {
            k: shares[k].astype(F32)
            + swap(shares[k ^ distance].astype(BF16), "mp", mp, distance).astype(F32)
            for k in shares
            if not k & distance
        }
        distance *= 2
    return shares[0].astype(node_vectors.dtype)


def solution(mesh):
    return jax.shard_map(
        lambda *arrays: per_device(mesh, *arrays),
        mesh=mesh,
        in_specs=(
            P(("groups", "seq"), "mp"),
            P(),
            P(None, "mp"),
            P(None, "mp"),
            P(None, "mp"),
            P("mp"),
            P("mp", None),
        ),
        out_specs=P(("groups", "seq"), "mp"),
        check_vma=False,
    )
```

```python
import functools
import math

import jax
import jax.numpy as jnp
from jax import lax
from jax.experimental import pallas as pl
from jax.experimental.pallas import tpu as pltpu
from jax.sharding import PartitionSpec as P

F32, BF16 = jnp.float32, jnp.bfloat16
VMEM = pl.BlockSpec(memory_space=pltpu.VMEM)
HBM = pl.BlockSpec(memory_space=pltpu.HBM)
LANES = 128


def call(kernel, name, out_shape, operands, work=0, limit=16, specs=None, scratch=()):
    return pl.pallas_call(
        kernel,
        out_shape=out_shape,
        in_specs=specs or [VMEM] * len(operands),
        out_specs=[VMEM] * len(out_shape),
        scratch_shapes=scratch,
        compiler_params=pltpu.CompilerParams(vmem_limit_bytes=limit << 20),
        cost_estimate=pl.CostEstimate(flops=work, bytes_accessed=work // 64, transcendentals=0),
        name=name,
    )(*operands)


def swap(block, axis, count, distance):
    return lax.ppermute(block, axis, [(i, i ^ distance) for i in range(count)])


def after(value, *others):
    return lax.optimization_barrier((value, *others))[0]


def parity():
    return lax.rem(lax.axis_index("seq"), 2)


def prepare_kernel(mp, gain_ref, probe_ref, lookup_ref, content_ref, exit_ref, *refs):
    weight_refs, (sums_ref, gain_out_ref, own_ref, twin_ref, far_ref) = refs[:3], refs[3:8]
    rows_ref, sems, gain_sem, exit_sems = refs[8:]
    me = lax.axis_index("mp")
    depth, cols = probe_ref.shape
    parts = sems.shape[0]
    chunk = depth // parts
    gain_copy = pltpu.make_async_copy(gain_ref, gain_out_ref, gain_sem)
    gain_copy.start()
    copies = []
    for c in range(parts):
        rows = pl.ds(c * chunk, chunk)
        copies.append([])
        for i, ref in enumerate((probe_ref, lookup_ref, content_ref)):
            copy = pltpu.make_async_copy(ref.at[rows, :], weight_refs[i].at[rows, :], sems.at[c, i])
            copy.start()
            copies[c].append(copy)
    half, deep, width = own_ref.shape
    mine = pl.ds(pl.multiple_of(parity() * deep, deep), deep)
    other = pl.ds(pl.multiple_of((1 - parity()) * deep, deep), deep)
    exits = []
    for j, (to_ref, rows, distance) in enumerate(
        ((own_ref, other, 0), (twin_ref, mine, 1), (far_ref, slice(None), half))
    ):
        for k in range(half):
            columns = pl.ds(pl.multiple_of((me ^ distance ^ k) * width, width), width)
            exits.append(
                pltpu.make_async_copy(exit_ref.at[rows, columns], to_ref.at[k], exit_sems.at[j * half + k])
            )
            exits[-1].start()
    gain_copy.wait()
    gain = gain_out_ref[...]
    high = gain.astype(BF16)
    rows_ref[...] = jnp.zeros_like(rows_ref)
    rows_ref[0:1, :] = high
    rows_ref[16:17, :] = (gain - high.astype(F32)).astype(BF16)
    for c in range(parts):
        for copy in copies[c]:
            copy.wait()
        span = pl.ds(c * chunk, chunk)
        for i, ref in enumerate(weight_refs):
            part = jnp.dot(rows_ref[:, span], ref[span, :], preferred_element_type=F32)
            part = part[0:8, :] + part[16:24, :]
            if c == 0:
                sums_ref[i] = part
            else:
                sums_ref[i] += part
    for copy in exits:
        copy.wait()


def prepare(mp, gain, probe, lookup, content, exit_matrix):
    depth, cols = probe.shape
    deep, wide = exit_matrix.shape
    parts = 4
    half, stack = (pltpu.VMEM((mp // 2, d, wide // mp), BF16) for d in (deep // 2, deep))
    probe, lookup, content, sums, gain, own, twin, far = call(
        functools.partial(prepare_kernel, mp),
        "prepare",
        [pltpu.VMEM((depth, cols), BF16)] * 3
        + [pltpu.VMEM((3, 8, cols), F32), pltpu.VMEM((1, depth), F32), half, half, stack],
        [
            pltpu.with_memory_space_constraint(w, pltpu.HBM)
            for w in (gain[None, :], probe, lookup, content, exit_matrix)
        ],
        work=48 * depth * cols,
        specs=[HBM] * 5,
        scratch=[
            pltpu.VMEM((32, depth), BF16),
            pltpu.SemaphoreType.DMA((parts, 3)),
            pltpu.SemaphoreType.DMA,
            pltpu.SemaphoreType.DMA((3 * mp // 2,)),
        ],
    )
    return (probe, lookup, content), sums, gain, own, twin, far


def matmul(blocks, places, weight_ref):
    me = lax.axis_index("mp")
    total = None
    for k, block in zip(places, blocks):
        depth = block.shape[1]
        w = weight_ref[pl.ds(pl.multiple_of((me ^ k) * depth, depth), depth), :]
        part = jnp.dot(block[...], w, preferred_element_type=F32)
        total = part if total is None else total + part
    return total


def take_in(blocks, places, shift, gain_ref, weight_refs):
    me = lax.axis_index("mp")
    one, two, scaled = 0.0, 0.0, []
    for k, block in zip(places, blocks):
        width = block.shape[1]
        gain = gain_ref[0:1, pl.ds(pl.multiple_of((me ^ k) * width, width), width)]
        moved = block[...].astype(F32) - shift
        scaled.append((moved * gain).astype(BF16))
        one += jnp.sum(moved, axis=1, keepdims=True)
        two += jnp.sum(moved * moved, axis=1, keepdims=True)
    return one, two, [matmul(scaled, places, ref) for ref in weight_refs]


def early_kernel(places, *refs):
    count = len(places)
    blocks = refs[:count]
    weight_refs, (gain_ref, factor_ref, stats_ref), product_refs, (factor_out_ref,) = (
        refs[count : count + 3],
        refs[count + 3 : count + 6],
        refs[count + 6 : count + 9],
        refs[count + 9 :],
    )
    factor_out_ref[...] = factor_ref[...]
    shift = jnp.mean(blocks[0][...].astype(F32), axis=1, keepdims=True)
    one, two, products = take_in(blocks, places, shift, gain_ref, weight_refs)
    for ref, product in zip(product_refs, products):
        ref[...] = product
    for i, value in enumerate((shift, one, two)):
        stats_ref[i] = jnp.broadcast_to(value, stats_ref.shape[1:])


def late_kernel(places, depth, *refs):
    count = len(places)
    blocks, refs = refs[:count], refs[count:]
    weight_refs, (gain_ref, sums_ref, stats_ref, factor_ref), product_refs = refs[:3], refs[3:7], refs[7:10]
    out_refs = refs[10:]
    one, two, products = take_in(blocks, places, stats_ref[0, :, 0:1], gain_ref, weight_refs)
    offset = (one + stats_ref[1, :, 0:1]) / depth
    scale = lax.rsqrt((two + stats_ref[2, :, 0:1]) / depth - offset * offset + 1e-05)
    first = parity() == 0
    parts = []
    for i, (product, ref) in enumerate(zip(products, product_refs)):
        product = product + ref[...]
        product = scale * (product - offset * sums_ref[i, 0:1, :])
        if i == 0:
            product = product * factor_ref[...]
        half = product.shape[1] // 2
        low, high = product[:, :half], product[:, half:]
        parts.append([jnp.where(first, *v).astype(BF16) for v in ((low, high), (high, low))])
    for g in range(2):
        for ref in out_refs[2 * g : 2 * g + 2]:
            for i in range(2):
                for h in range(half // LANES):
                    part = parts[i + 1][g][:, h * LANES : (h + 1) * LANES]
                    ref[:, pl.ds((2 * h + i) * LANES, LANES)] = part
        out_refs[2 * g + 1][:, pl.ds(2 * half, half)] = parts[0][g]


def project(blocks, places, weights, sums, gain, factor):
    rows, width = blocks[0].shape
    cols = weights[0].shape[1]
    count = len(blocks)
    product = pltpu.VMEM((rows, cols), F32)
    stats, *products, factor = call(
        functools.partial(early_kernel, places[:-1]),
        "early",
        [pltpu.VMEM((3, rows, LANES), F32), product, product, product, pltpu.VMEM(factor.shape, F32)],
        [*blocks[:-1], *weights, gain, factor],
        work=16 * rows * weights[0].size,
    )
    pair = pltpu.VMEM((rows, cols), BF16)
    return call(
        functools.partial(late_kernel, places[-1:], count * width),
        "late",
        [pair, pltpu.VMEM((rows, 3 * cols // 2), BF16)] * 2,
        [blocks[-1], *weights, gain, sums, stats, factor, *products],
    )


def merge_kernel(*refs):
    rows = refs[0].shape[0]
    for i, ref in enumerate(refs[:-1]):
        refs[-1][pl.ds(i * rows, rows), :] = ref[...]


def attend_kernel(*refs):
    bundles, blocks, out_refs = refs[:2], refs[:3], refs[3:]
    rows, half = out_refs[0].shape
    for h in range(half // LANES):
        q = jnp.concatenate([b[:, pl.ds(2 * half + h * LANES, LANES)] for b in bundles], axis=0)
        scores = [
            lax.dot_general(
                q, b[:, pl.ds(2 * h * LANES, LANES)], (((1,), (1,)), ((), ())), preferred_element_type=F32
            )
            for b in blocks
        ]
        top = functools.reduce(jnp.maximum, [jnp.max(s, axis=1, keepdims=True) for s in scores])
        weights = [jnp.exp2(s - top) for s in scores]
        weighted = sum(
            jnp.dot(
                w.astype(BF16), b[:, pl.ds((2 * h + 1) * LANES, LANES)], preferred_element_type=F32
            )
            for w, b in zip(weights, blocks)
        )
        total = sum(jnp.sum(w, axis=1, keepdims=True) for w in weights)
        out = (weighted / total).astype(BF16)
        for i, ref in enumerate(out_refs):
            ref[:, pl.ds(h * LANES, LANES)] = out[i * rows : (i + 1) * rows, :]


def attend(bundles, blocks):
    rows, wide = blocks[0].shape
    (merged,) = call(
        merge_kernel,
        "merge",
        [pltpu.VMEM((len(blocks) * rows, wide), BF16)],
        blocks,
        work=30000 * rows * wide * len(blocks),
    )
    (beside,) = call(
        merge_kernel,
        "hold",
        [pltpu.VMEM(bundles[1].shape, BF16)],
        bundles[1:],
        work=30000 * rows * wide,
    )
    return call(
        attend_kernel,
        "attend",
        [pltpu.VMEM((rows, wide // 2), BF16)] * 2,
        [bundles[0], beside, merged],
        limit=56 if merged.shape[0] > 2048 else 16,
    )


def own_kernel(x_ref, mixed_ref, exit_ref, *out_refs):
    for k, ref in enumerate(out_refs):
        part = jnp.dot(mixed_ref[...], exit_ref[k], preferred_element_type=F32)
        ref[...] = part + x_ref[...].astype(F32) if k == 0 else part


def add_kernel(which, halves, *refs):
    count, values = len(which), len(halves)
    for i, k in enumerate(which):
        total = refs[2 * values + i][...]
        for j, half in enumerate(halves):
            deep = refs[j].shape[1]
            rows = slice(None)
            if half is not None:
                at = 1 - parity() if half else parity()
                rows = pl.ds(pl.multiple_of(at * deep, deep), deep)
            total += jnp.dot(refs[j][...], refs[values + j][k, rows, :], preferred_element_type=F32)
        out_ref = refs[2 * values + count + i]
        out_ref[...] = total.astype(out_ref.dtype)


def per_device(mesh, node_vectors, gain, probe, lookup, content, softness, exit_matrix):
    mp, seq = mesh.shape["mp"], mesh.shape["seq"]
    heads = softness.shape[0]
    cols = probe.shape[1]
    span = cols // heads
    top = mp // 2
    step = top | 1
    factor = jnp.repeat(softness * (math.log2(math.e) / math.sqrt(span)), span)[None, :]

    weights, sums, gains, own, twin, far = prepare(mp, gain, probe, lookup, content, exit_matrix)
    blocks, distance = {0: node_vectors}, top
    while distance:
        new = {k ^ distance: swap(b, "mp", mp, distance) for k, b in blocks.items()}
        if distance == top:
            new, sums = lax.optimization_barrier((new, sums))
        blocks.update(new)
        distance //= 2
    places = range(mp)
    mine, mine_bundle, other, other_bundle = project(
        [blocks[k] for k in places], places, weights, sums, gains, factor
    )
    theirs = swap(far, "mp", mp, top)

    both = ("seq", "mp")
    found = {}
    for k in range(2, seq):
        found[k] = swap(other if k % 2 else mine, both, seq * mp, k * mp + 1)
    bundles = [swap(after(mine_bundle, found[2]), "mp", mp, 1), swap(other_bundle, both, seq * mp, mp + 1)]
    twins = swap(after(twin, found[2]), "mp", mp, 1)
    mixed, mixed_beside = attend(bundles, [found[k] for k in range(2, seq)])

    rows, width = node_vectors.shape
    product, half = pltpu.VMEM((rows, width), F32), pltpu.VMEM((rows, width), BF16)
    across = swap(mixed, both, seq * mp, step)
    beside = swap(mixed_beside, both, seq * mp, mp + 1)
    corner = swap(mixed_beside, both, seq * mp, mp + step)
    parts = call(
        own_kernel, "own", [product] * top, [node_vectors, mixed, twins], work=1 * rows * own.size
    )
    parts = call(
        functools.partial(add_kernel, range(top), (0, 1)),
        "crossed",
        [product] * top,
        [across, corner, theirs, theirs, *parts],
        work=64 * rows * own.size,
    )
    sent = call(
        functools.partial(add_kernel, range(1, top), (None,)),
        "sent",
        [half] * (top - 1),
        [beside, own, *parts[1:]],
    )
    (kept,) = call(
        functools.partial(add_kernel, range(1), (None,)),
        "kept",
        [product],
        [beside, own, parts[0]],
        work=64 * rows * own.size,
    )
    shares = {0: kept, **{k: sent[k - 1] for k in range(1, top)}}
    distance = 1
    while distance < top:
        shares = {
            k: shares[k].astype(F32)
            + swap(shares[k ^ distance].astype(BF16), "mp", mp, distance).astype(F32)
            for k in shares
            if not k & distance
        }
        distance *= 2
    return shares[0].astype(node_vectors.dtype)


def solution(mesh):
    return jax.shard_map(
        lambda *arrays: per_device(mesh, *arrays),
        mesh=mesh,
        in_specs=(
            P(("groups", "seq"), "mp"),
            P(),
            P(None, "mp"),
            P(None, "mp"),
            P(None, "mp"),
            P("mp"),
            P("mp", None),
        ),
        out_specs=P(("groups", "seq"), "mp"),
        check_vma=False,
    )
```

```python
import functools
import math

import jax
import jax.numpy as jnp
from jax import lax
from jax.experimental import pallas as pl
from jax.experimental.pallas import tpu as pltpu
from jax.sharding import PartitionSpec as P

F32, BF16 = jnp.float32, jnp.bfloat16
VMEM = pl.BlockSpec(memory_space=pltpu.VMEM)
HBM = pl.BlockSpec(memory_space=pltpu.HBM)
LANES = 128


def call(kernel, name, out_shape, operands, work=0, limit=16, specs=None, scratch=()):
    return pl.pallas_call(
        kernel,
        out_shape=out_shape,
        in_specs=specs or [VMEM] * len(operands),
        out_specs=[VMEM] * len(out_shape),
        scratch_shapes=scratch,
        compiler_params=pltpu.CompilerParams(vmem_limit_bytes=limit << 20),
        cost_estimate=pl.CostEstimate(flops=work, bytes_accessed=work // 64, transcendentals=0),
        name=name,
    )(*operands)


def swap(block, axis, count, distance):
    return lax.ppermute(block, axis, [(i, i ^ distance) for i in range(count)])


def after(value, *others):
    return lax.optimization_barrier((value, *others))[0]


def parity():
    return lax.rem(lax.axis_index("seq"), 2)


def prepare_kernel(mp, gain_ref, probe_ref, lookup_ref, content_ref, exit_ref, *refs):
    weight_refs, (sums_ref, gain_out_ref, own_ref, twin_ref, far_ref) = refs[:3], refs[3:8]
    rows_ref, sems, gain_sem, exit_sems = refs[8:]
    me = lax.axis_index("mp")
    depth, cols = probe_ref.shape
    parts = sems.shape[0]
    chunk = depth // parts
    gain_copy = pltpu.make_async_copy(gain_ref, gain_out_ref, gain_sem)
    gain_copy.start()
    copies = []
    for c in range(parts):
        rows = pl.ds(c * chunk, chunk)
        copies.append([])
        for i, ref in enumerate((probe_ref, lookup_ref, content_ref)):
            copy = pltpu.make_async_copy(ref.at[rows, :], weight_refs[i].at[rows, :], sems.at[c, i])
            copy.start()
            copies[c].append(copy)
    half, deep, width = own_ref.shape
    mine = pl.ds(pl.multiple_of(parity() * deep, deep), deep)
    other = pl.ds(pl.multiple_of((1 - parity()) * deep, deep), deep)
    exits = []
    for j, (to_ref, rows, distance) in enumerate(
        ((own_ref, other, 0), (twin_ref, mine, 1), (far_ref, slice(None), half))
    ):
        for k in range(half):
            columns = pl.ds(pl.multiple_of((me ^ distance ^ k) * width, width), width)
            exits.append(
                pltpu.make_async_copy(exit_ref.at[rows, columns], to_ref.at[k], exit_sems.at[j * half + k])
            )
            exits[-1].start()
    gain_copy.wait()
    gain = gain_out_ref[...]
    high = gain.astype(BF16)
    rows_ref[...] = jnp.zeros_like(rows_ref)
    rows_ref[0:1, :] = high
    rows_ref[16:17, :] = (gain - high.astype(F32)).astype(BF16)
    for c in range(parts):
        for copy in copies[c]:
            copy.wait()
        span = pl.ds(c * chunk, chunk)
        for i, ref in enumerate(weight_refs):
            part = jnp.dot(rows_ref[:, span], ref[span, :], preferred_element_type=F32)
            part = part[0:8, :] + part[16:24, :]
            if c == 0:
                sums_ref[i] = part
            else:
                sums_ref[i] += part
    for copy in exits:
        copy.wait()


def prepare(mp, gain, probe, lookup, content, exit_matrix):
    depth, cols = probe.shape
    deep, wide = exit_matrix.shape
    parts = 4
    half, stack = (pltpu.VMEM((mp // 2, d, wide // mp), BF16) for d in (deep // 2, deep))
    probe, lookup, content, sums, gain, own, twin, far = call(
        functools.partial(prepare_kernel, mp),
        "prepare",
        [pltpu.VMEM((depth, cols), BF16)] * 3
        + [pltpu.VMEM((3, 8, cols), F32), pltpu.VMEM((1, depth), F32), half, half, stack],
        [
            pltpu.with_memory_space_constraint(w, pltpu.HBM)
            for w in (gain[None, :], probe, lookup, content, exit_matrix)
        ],
        work=48 * depth * cols,
        specs=[HBM] * 5,
        scratch=[
            pltpu.VMEM((32, depth), BF16),
            pltpu.SemaphoreType.DMA((parts, 3)),
            pltpu.SemaphoreType.DMA,
            pltpu.SemaphoreType.DMA((3 * mp // 2,)),
        ],
    )
    return (probe, lookup, content), sums, gain, own, twin, far


def matmul(blocks, places, weight_ref):
    me = lax.axis_index("mp")
    total = None
    for k, block in zip(places, blocks):
        depth = block.shape[1]
        w = weight_ref[pl.ds(pl.multiple_of((me ^ k) * depth, depth), depth), :]
        part = jnp.dot(block[...], w, preferred_element_type=F32)
        total = part if total is None else total + part
    return total


def take_in(blocks, places, shift, gain_ref, weight_refs):
    me = lax.axis_index("mp")
    one, two, scaled = 0.0, 0.0, []
    for k, block in zip(places, blocks):
        width = block.shape[1]
        gain = gain_ref[0:1, pl.ds(pl.multiple_of((me ^ k) * width, width), width)]
        moved = block[...].astype(F32) - shift
        scaled.append((moved * gain).astype(BF16))
        one += jnp.sum(moved, axis=1, keepdims=True)
        two += jnp.sum(moved * moved, axis=1, keepdims=True)
    return one, two, [matmul(scaled, places, ref) for ref in weight_refs]


def early_kernel(places, *refs):
    count = len(places)
    blocks = refs[:count]
    weight_refs, (gain_ref, factor_ref, stats_ref), product_refs, (factor_out_ref,) = (
        refs[count : count + 3],
        refs[count + 3 : count + 6],
        refs[count + 6 : count + 9],
        refs[count + 9 :],
    )
    factor_out_ref[...] = factor_ref[...]
    shift = jnp.mean(blocks[0][...].astype(F32), axis=1, keepdims=True)
    one, two, products = take_in(blocks, places, shift, gain_ref, weight_refs)
    for ref, product in zip(product_refs, products):
        ref[...] = product
    for i, value in enumerate((shift, one, two)):
        stats_ref[i] = jnp.broadcast_to(value, stats_ref.shape[1:])


def late_kernel(places, depth, *refs):
    count = len(places)
    blocks, refs = refs[:count], refs[count:]
    weight_refs, (gain_ref, sums_ref, stats_ref, factor_ref), product_refs = refs[:3], refs[3:7], refs[7:10]
    out_refs = refs[10:]
    one, two, products = take_in(blocks, places, stats_ref[0, :, 0:1], gain_ref, weight_refs)
    offset = (one + stats_ref[1, :, 0:1]) / depth
    scale = lax.rsqrt((two + stats_ref[2, :, 0:1]) / depth - offset * offset + 1e-05)
    first = parity() == 0
    parts = []
    for i, (product, ref) in enumerate(zip(products, product_refs)):
        product = product + ref[...]
        product = scale * (product - offset * sums_ref[i, 0:1, :])
        if i == 0:
            product = product * factor_ref[...]
        half = product.shape[1] // 2
        low, high = product[:, :half], product[:, half:]
        parts.append([jnp.where(first, *v).astype(BF16) for v in ((low, high), (high, low))])
    for g in range(2):
        for ref in out_refs[2 * g : 2 * g + 2]:
            for i in range(2):
                for h in range(half // LANES):
                    part = parts[i + 1][g][:, h * LANES : (h + 1) * LANES]
                    ref[:, pl.ds((2 * h + i) * LANES, LANES)] = part
        out_refs[2 * g + 1][:, pl.ds(2 * half, half)] = parts[0][g]


def project(blocks, places, weights, sums, gain, factor):
    rows, width = blocks[0].shape
    cols = weights[0].shape[1]
    count = len(blocks)
    product = pltpu.VMEM((rows, cols), F32)
    stats, *products, factor = call(
        functools.partial(early_kernel, places[:-1]),
        "early",
        [pltpu.VMEM((3, rows, LANES), F32), product, product, product, pltpu.VMEM(factor.shape, F32)],
        [*blocks[:-1], *weights, gain, factor],
        work=16 * rows * weights[0].size,
    )
    pair = pltpu.VMEM((rows, cols), BF16)
    return call(
        functools.partial(late_kernel, places[-1:], count * width),
        "late",
        [pair, pltpu.VMEM((rows, 3 * cols // 2), BF16)] * 2,
        [blocks[-1], *weights, gain, sums, stats, factor, *products],
    )


def merge_kernel(*refs):
    rows = refs[0].shape[0]
    for i, ref in enumerate(refs[:-1]):
        refs[-1][pl.ds(i * rows, rows), :] = ref[...]


def attend_kernel(*refs):
    bundles, blocks, out_refs = refs[:2], refs[:3], refs[3:]
    rows, half = out_refs[0].shape
    for h in range(half // LANES):
        q = jnp.concatenate([b[:, pl.ds(2 * half + h * LANES, LANES)] for b in bundles], axis=0)
        scores = [
            lax.dot_general(
                q, b[:, pl.ds(2 * h * LANES, LANES)], (((1,), (1,)), ((), ())), preferred_element_type=F32
            )
            for b in blocks
        ]
        top = functools.reduce(jnp.maximum, [jnp.max(s, axis=1, keepdims=True) for s in scores])
        weights = [jnp.exp2(s - top) for s in scores]
        weighted = sum(
            jnp.dot(
                w.astype(BF16), b[:, pl.ds((2 * h + 1) * LANES, LANES)], preferred_element_type=F32
            )
            for w, b in zip(weights, blocks)
        )
        total = sum(jnp.sum(w, axis=1, keepdims=True) for w in weights)
        out = (weighted / total).astype(BF16)
        for i, ref in enumerate(out_refs):
            ref[:, pl.ds(h * LANES, LANES)] = out[i * rows : (i + 1) * rows, :]


def attend(bundles, blocks):
    rows, wide = blocks[0].shape
    (merged,) = call(
        merge_kernel,
        "merge",
        [pltpu.VMEM((len(blocks) * rows, wide), BF16)],
        blocks,
        work=30000 * rows * wide * len(blocks),
    )
    (beside,) = call(
        merge_kernel,
        "hold",
        [pltpu.VMEM(bundles[1].shape, BF16)],
        bundles[1:],
        work=30000 * rows * wide,
    )
    return call(
        attend_kernel,
        "attend",
        [pltpu.VMEM((rows, wide // 2), BF16)] * 2,
        [bundles[0], beside, merged],
        limit=56 if merged.shape[0] > 2048 else 16,
    )


def own_kernel(x_ref, mixed_ref, exit_ref, *out_refs):
    for k, ref in enumerate(out_refs):
        part = jnp.dot(mixed_ref[...], exit_ref[k], preferred_element_type=F32)
        ref[...] = part + x_ref[...].astype(F32) if k == 0 else part


def add_kernel(which, halves, *refs):
    count, values = len(which), len(halves)
    for i, k in enumerate(which):
        total = refs[2 * values + i][...]
        for j, half in enumerate(halves):
            deep = refs[j].shape[1]
            rows = slice(None)
            if half is not None:
                at = 1 - parity() if half else parity()
                rows = pl.ds(pl.multiple_of(at * deep, deep), deep)
            total += jnp.dot(refs[j][...], refs[values + j][k, rows, :], preferred_element_type=F32)
        out_ref = refs[2 * values + count + i]
        out_ref[...] = total.astype(out_ref.dtype)


def per_device(mesh, node_vectors, gain, probe, lookup, content, softness, exit_matrix):
    mp, seq = mesh.shape["mp"], mesh.shape["seq"]
    heads = softness.shape[0]
    cols = probe.shape[1]
    span = cols // heads
    top = mp // 2
    step = top | 1
    factor = jnp.repeat(softness * (math.log2(math.e) / math.sqrt(span)), span)[None, :]

    weights, sums, gains, own, twin, far = prepare(mp, gain, probe, lookup, content, exit_matrix)
    blocks, distance = {0: node_vectors}, top
    while distance:
        new = {k ^ distance: swap(b, "mp", mp, distance) for k, b in blocks.items()}
        if distance == top:
            new, sums = lax.optimization_barrier((new, sums))
        blocks.update(new)
        distance //= 2
    places = range(mp)
    mine, mine_bundle, other, other_bundle = project(
        [blocks[k] for k in places], places, weights, sums, gains, factor
    )
    theirs = swap(far, "mp", mp, top)

    both = ("seq", "mp")
    found = {}
    for k in range(2, seq):
        found[k] = swap(other if k % 2 else mine, both, seq * mp, k * mp + 1)
    bundles = [swap(after(mine_bundle, found[2]), "mp", mp, 1), swap(other_bundle, both, seq * mp, mp + 1)]
    twins = swap(after(twin, found[2]), "mp", mp, 1)
    mixed, mixed_beside = attend(bundles, [found[k] for k in range(2, seq)])

    rows, width = node_vectors.shape
    product, half = pltpu.VMEM((rows, width), F32), pltpu.VMEM((rows, width), BF16)
    across = swap(mixed, both, seq * mp, step)
    beside = swap(mixed_beside, both, seq * mp, mp + 1)
    corner = swap(mixed_beside, both, seq * mp, mp + step)
    parts = call(
        own_kernel, "own", [product] * top, [node_vectors, mixed, twins], work=1 * rows * own.size
    )
    crossed = call(
        functools.partial(add_kernel, range(1, top), (1, 0)),
        "crossed",
        [product] * (top - 1),
        [corner, across, theirs, theirs, *parts[1:]],
        work=64 * rows * own.size,
    )
    sent = call(
        functools.partial(add_kernel, range(1, top), (None,)),
        "sent",
        [half] * (top - 1),
        [beside, own, *crossed],
    )
    (kept,) = call(
        functools.partial(add_kernel, range(1), (1, 0, None)),
        "kept",
        [product],
        [corner, across, beside, theirs, theirs, own, parts[0]],
        work=64 * rows * own.size,
    )
    shares = {0: kept, **{k: sent[k - 1] for k in range(1, top)}}
    distance = 1
    while distance < top:
        shares = {
            k: shares[k].astype(F32)
            + swap(shares[k ^ distance].astype(BF16), "mp", mp, distance).astype(F32)
            for k in shares
            if not k & distance
        }
        distance *= 2
    return shares[0].astype(node_vectors.dtype)


def solution(mesh):
    return jax.shard_map(
        lambda *arrays: per_device(mesh, *arrays),
        mesh=mesh,
        in_specs=(
            P(("groups", "seq"), "mp"),
            P(),
            P(None, "mp"),
            P(None, "mp"),
            P(None, "mp"),
            P("mp"),
            P("mp", None),
        ),
        out_specs=P(("groups", "seq"), "mp"),
        check_vma=False,
    )
```

```python
import functools
import math

import jax
import jax.numpy as jnp
from jax import lax
from jax.experimental import pallas as pl
from jax.experimental.pallas import tpu as pltpu
from jax.sharding import PartitionSpec as P

F32, BF16 = jnp.float32, jnp.bfloat16
VMEM = pl.BlockSpec(memory_space=pltpu.VMEM)
HBM = pl.BlockSpec(memory_space=pltpu.HBM)
LANES = 128


def call(kernel, name, out_shape, operands, work=0, limit=16, specs=None, scratch=()):
    return pl.pallas_call(
        kernel,
        out_shape=out_shape,
        in_specs=specs or [VMEM] * len(operands),
        out_specs=[VMEM] * len(out_shape),
        scratch_shapes=scratch,
        compiler_params=pltpu.CompilerParams(vmem_limit_bytes=limit << 20),
        cost_estimate=pl.CostEstimate(flops=work, bytes_accessed=work // 64, transcendentals=0),
        name=name,
    )(*operands)


def swap(block, axis, count, distance):
    return lax.ppermute(block, axis, [(i, i ^ distance) for i in range(count)])


def after(value, *others):
    return lax.optimization_barrier((value, *others))[0]


def parity():
    return lax.rem(lax.axis_index("seq"), 2)


def prepare_kernel(mp, gain_ref, probe_ref, lookup_ref, content_ref, exit_ref, *refs):
    weight_refs, (sums_ref, gain_out_ref, own_ref, twin_ref, far_ref) = refs[:3], refs[3:8]
    rows_ref, sems, gain_sem, exit_sems = refs[8:]
    me = lax.axis_index("mp")
    depth, cols = probe_ref.shape
    parts = sems.shape[0]
    chunk = depth // parts
    gain_copy = pltpu.make_async_copy(gain_ref, gain_out_ref, gain_sem)
    gain_copy.start()
    copies = []
    for c in range(parts):
        rows = pl.ds(c * chunk, chunk)
        copies.append([])
        for i, ref in enumerate((probe_ref, lookup_ref, content_ref)):
            copy = pltpu.make_async_copy(ref.at[rows, :], weight_refs[i].at[rows, :], sems.at[c, i])
            copy.start()
            copies[c].append(copy)
    half, deep, width = own_ref.shape
    mine = pl.ds(pl.multiple_of(parity() * deep, deep), deep)
    other = pl.ds(pl.multiple_of((1 - parity()) * deep, deep), deep)
    exits = []
    for j, (to_ref, rows, distance) in enumerate(
        ((own_ref, other, 0), (twin_ref, mine, 1), (far_ref, slice(None), half))
    ):
        for k in range(half):
            columns = pl.ds(pl.multiple_of((me ^ distance ^ k) * width, width), width)
            exits.append(
                pltpu.make_async_copy(exit_ref.at[rows, columns], to_ref.at[k], exit_sems.at[j * half + k])
            )
            exits[-1].start()
    gain_copy.wait()
    gain = gain_out_ref[...]
    high = gain.astype(BF16)
    rows_ref[...] = jnp.zeros_like(rows_ref)
    rows_ref[0:1, :] = high
    rows_ref[16:17, :] = (gain - high.astype(F32)).astype(BF16)
    for c in range(parts):
        for copy in copies[c]:
            copy.wait()
        span = pl.ds(c * chunk, chunk)
        for i, ref in enumerate(weight_refs):
            part = jnp.dot(rows_ref[:, span], ref[span, :], preferred_element_type=F32)
            part = part[0:8, :] + part[16:24, :]
            if c == 0:
                sums_ref[i] = part
            else:
                sums_ref[i] += part
    for copy in exits:
        copy.wait()


def prepare(mp, gain, probe, lookup, content, exit_matrix):
    depth, cols = probe.shape
    deep, wide = exit_matrix.shape
    parts = 2
    half, stack = (pltpu.VMEM((mp // 2, d, wide // mp), BF16) for d in (deep // 2, deep))
    probe, lookup, content, sums, gain, own, twin, far = call(
        functools.partial(prepare_kernel, mp),
        "prepare",
        [pltpu.VMEM((depth, cols), BF16)] * 3
        + [pltpu.VMEM((3, 8, cols), F32), pltpu.VMEM((1, depth), F32), half, half, stack],
        [
            pltpu.with_memory_space_constraint(w, pltpu.HBM)
            for w in (gain[None, :], probe, lookup, content, exit_matrix)
        ],
        work=48 * depth * cols,
        specs=[HBM] * 5,
        scratch=[
            pltpu.VMEM((32, depth), BF16),
            pltpu.SemaphoreType.DMA((parts, 3)),
            pltpu.SemaphoreType.DMA,
            pltpu.SemaphoreType.DMA((3 * mp // 2,)),
        ],
    )
    return (probe, lookup, content), sums, gain, own, twin, far


def matmul(blocks, places, weight_ref):
    me = lax.axis_index("mp")
    total = None
    for k, block in zip(places, blocks):
        depth = block.shape[1]
        w = weight_ref[pl.ds(pl.multiple_of((me ^ k) * depth, depth), depth), :]
        part = jnp.dot(block[...], w, preferred_element_type=F32)
        total = part if total is None else total + part
    return total


def take_in(blocks, places, shift, gain_ref, weight_refs):
    me = lax.axis_index("mp")
    one, two, scaled = 0.0, 0.0, []
    for k, block in zip(places, blocks):
        width = block.shape[1]
        gain = gain_ref[0:1, pl.ds(pl.multiple_of((me ^ k) * width, width), width)]
        moved = block[...].astype(F32) - shift
        scaled.append((moved * gain).astype(BF16))
        one += jnp.sum(moved, axis=1, keepdims=True)
        two += jnp.sum(moved * moved, axis=1, keepdims=True)
    return one, two, [matmul(scaled, places, ref) for ref in weight_refs]


def early_kernel(places, *refs):
    count = len(places)
    blocks = refs[:count]
    weight_refs, (gain_ref, factor_ref, stats_ref), product_refs, (factor_out_ref,) = (
        refs[count : count + 3],
        refs[count + 3 : count + 6],
        refs[count + 6 : count + 9],
        refs[count + 9 :],
    )
    factor_out_ref[...] = factor_ref[...]
    shift = jnp.mean(blocks[0][...].astype(F32), axis=1, keepdims=True)
    one, two, products = take_in(blocks, places, shift, gain_ref, weight_refs)
    for ref, product in zip(product_refs, products):
        ref[...] = product
    for i, value in enumerate((shift, one, two)):
        stats_ref[i] = jnp.broadcast_to(value, stats_ref.shape[1:])


def late_kernel(places, depth, *refs):
    count = len(places)
    blocks, refs = refs[:count], refs[count:]
    weight_refs, (gain_ref, sums_ref, stats_ref, factor_ref), product_refs = refs[:3], refs[3:7], refs[7:10]
    out_refs = refs[10:]
    one, two, products = take_in(blocks, places, stats_ref[0, :, 0:1], gain_ref, weight_refs)
    offset = (one + stats_ref[1, :, 0:1]) / depth
    scale = lax.rsqrt((two + stats_ref[2, :, 0:1]) / depth - offset * offset + 1e-05)
    first = parity() == 0
    parts = []
    for i, (product, ref) in enumerate(zip(products, product_refs)):
        product = product + ref[...]
        product = scale * (product - offset * sums_ref[i, 0:1, :])
        if i == 0:
            product = product * factor_ref[...]
        half = product.shape[1] // 2
        low, high = product[:, :half], product[:, half:]
        parts.append([jnp.where(first, *v).astype(BF16) for v in ((low, high), (high, low))])
    for g in range(2):
        for ref in out_refs[2 * g : 2 * g + 2]:
            for i in range(2):
                for h in range(half // LANES):
                    part = parts[i + 1][g][:, h * LANES : (h + 1) * LANES]
                    ref[:, pl.ds((2 * h + i) * LANES, LANES)] = part
        out_refs[2 * g + 1][:, pl.ds(2 * half, half)] = parts[0][g]


def project(blocks, places, weights, sums, gain, factor):
    rows, width = blocks[0].shape
    cols = weights[0].shape[1]
    count = len(blocks)
    product = pltpu.VMEM((rows, cols), F32)
    stats, *products, factor = call(
        functools.partial(early_kernel, places[:-1]),
        "early",
        [pltpu.VMEM((3, rows, LANES), F32), product, product, product, pltpu.VMEM(factor.shape, F32)],
        [*blocks[:-1], *weights, gain, factor],
        work=16 * rows * weights[0].size,
    )
    pair = pltpu.VMEM((rows, cols), BF16)
    return call(
        functools.partial(late_kernel, places[-1:], count * width),
        "late",
        [pair, pltpu.VMEM((rows, 3 * cols // 2), BF16)] * 2,
        [blocks[-1], *weights, gain, sums, stats, factor, *products],
    )


def merge_kernel(*refs):
    rows = refs[0].shape[0]
    for i, ref in enumerate(refs[:-1]):
        refs[-1][pl.ds(i * rows, rows), :] = ref[...]


def attend_kernel(*refs):
    bundles, blocks, out_refs = refs[:2], refs[:3], refs[3:]
    rows, half = out_refs[0].shape
    for h in range(half // LANES):
        q = jnp.concatenate([b[:, pl.ds(2 * half + h * LANES, LANES)] for b in bundles], axis=0)
        scores = [
            lax.dot_general(
                q, b[:, pl.ds(2 * h * LANES, LANES)], (((1,), (1,)), ((), ())), preferred_element_type=F32
            )
            for b in blocks
        ]
        top = functools.reduce(jnp.maximum, [jnp.max(s, axis=1, keepdims=True) for s in scores])
        weights = [jnp.exp2(s - top) for s in scores]
        weighted = sum(
            jnp.dot(
                w.astype(BF16), b[:, pl.ds((2 * h + 1) * LANES, LANES)], preferred_element_type=F32
            )
            for w, b in zip(weights, blocks)
        )
        total = sum(jnp.sum(w, axis=1, keepdims=True) for w in weights)
        out = (weighted / total).astype(BF16)
        for i, ref in enumerate(out_refs):
            ref[:, pl.ds(h * LANES, LANES)] = out[i * rows : (i + 1) * rows, :]


def attend(bundles, blocks):
    rows, wide = blocks[0].shape
    (merged,) = call(
        merge_kernel,
        "merge",
        [pltpu.VMEM((len(blocks) * rows, wide), BF16)],
        blocks,
        work=30000 * rows * wide * len(blocks),
    )
    (beside,) = call(
        merge_kernel,
        "hold",
        [pltpu.VMEM(bundles[1].shape, BF16)],
        bundles[1:],
        work=30000 * rows * wide,
    )
    return call(
        attend_kernel,
        "attend",
        [pltpu.VMEM((rows, wide // 2), BF16)] * 2,
        [bundles[0], beside, merged],
        limit=56 if merged.shape[0] > 2048 else 16,
    )


def own_kernel(x_ref, mixed_ref, exit_ref, *out_refs):
    for k, ref in enumerate(out_refs):
        part = jnp.dot(mixed_ref[...], exit_ref[k], preferred_element_type=F32)
        ref[...] = part + x_ref[...].astype(F32) if k == 0 else part


def add_kernel(which, halves, *refs):
    count, values = len(which), len(halves)
    for i, k in enumerate(which):
        total = refs[2 * values + i][...]
        for j, half in enumerate(halves):
            deep = refs[j].shape[1]
            rows = slice(None)
            if half is not None:
                at = 1 - parity() if half else parity()
                rows = pl.ds(pl.multiple_of(at * deep, deep), deep)
            total += jnp.dot(refs[j][...], refs[values + j][k, rows, :], preferred_element_type=F32)
        out_ref = refs[2 * values + count + i]
        out_ref[...] = total.astype(out_ref.dtype)


def per_device(mesh, node_vectors, gain, probe, lookup, content, softness, exit_matrix):
    mp, seq = mesh.shape["mp"], mesh.shape["seq"]
    heads = softness.shape[0]
    cols = probe.shape[1]
    span = cols // heads
    top = mp // 2
    step = top | 1
    factor = jnp.repeat(softness * (math.log2(math.e) / math.sqrt(span)), span)[None, :]

    weights, sums, gains, own, twin, far = prepare(mp, gain, probe, lookup, content, exit_matrix)
    blocks, distance = {0: node_vectors}, top
    while distance:
        new = {k ^ distance: swap(b, "mp", mp, distance) for k, b in blocks.items()}
        if distance == top:
            new, sums = lax.optimization_barrier((new, sums))
        blocks.update(new)
        distance //= 2
    places = range(mp)
    mine, mine_bundle, other, other_bundle = project(
        [blocks[k] for k in places], places, weights, sums, gains, factor
    )
    theirs = swap(far, "mp", mp, top)

    both = ("seq", "mp")
    found = {}
    for k in range(2, seq):
        found[k] = swap(other if k % 2 else mine, both, seq * mp, k * mp + 1)
    bundles = [swap(after(mine_bundle, found[2]), "mp", mp, 1), swap(other_bundle, both, seq * mp, mp + 1)]
    twins = swap(after(twin, found[2]), "mp", mp, 1)
    mixed, mixed_beside = attend(bundles, [found[k] for k in range(2, seq)])

    rows, width = node_vectors.shape
    product, half = pltpu.VMEM((rows, width), F32), pltpu.VMEM((rows, width), BF16)
    across = swap(mixed, both, seq * mp, step)
    beside = swap(mixed_beside, both, seq * mp, mp + 1)
    corner = swap(mixed_beside, both, seq * mp, mp + step)
    parts = call(
        own_kernel, "own", [product] * top, [node_vectors, mixed, twins], work=1 * rows * own.size
    )
    parts = call(
        functools.partial(add_kernel, range(top), (0, 1)),
        "crossed",
        [product] * top,
        [across, corner, theirs, theirs, *parts],
        work=64 * rows * own.size,
    )
    sent = call(
        functools.partial(add_kernel, range(1, top), (None,)),
        "sent",
        [half] * (top - 1),
        [beside, own, *parts[1:]],
    )
    (kept,) = call(
        functools.partial(add_kernel, range(1), (None,)),
        "kept",
        [product],
        [beside, own, parts[0]],
        work=64 * rows * own.size,
    )
    shares = {0: kept, **{k: sent[k - 1] for k in range(1, top)}}
    distance = 1
    while distance < top:
        shares = {
            k: shares[k].astype(F32)
            + swap(shares[k ^ distance].astype(BF16), "mp", mp, distance).astype(F32)
            for k in shares
            if not k & distance
        }
        distance *= 2
    return shares[0].astype(node_vectors.dtype)


def solution(mesh):
    return jax.shard_map(
        lambda *arrays: per_device(mesh, *arrays),
        mesh=mesh,
        in_specs=(
            P(("groups", "seq"), "mp"),
            P(),
            P(None, "mp"),
            P(None, "mp"),
            P(None, "mp"),
            P("mp"),
            P("mp", None),
        ),
        out_specs=P(("groups", "seq"), "mp"),
        check_vma=False,
    )
```
